256 devices in a mesh: seq: 8 (over y, x_hi), head: 32 (over x_lo, z, core).
Axes of the slice: x: 4 (x_hi: 2, x_lo: 2; x = x_hi * 2 + x_lo), y: 4, z: 8, core: 2. Of those that a mesh axis runs over, the one named last changes fastest.
Arguments:
- tokens: bfloat16 [4, 2048, 3072], P(None, ('seq', 'head')), may hold values from -6 to 6
- qkv_weight: bfloat16 [2, 32, 192, 3072], P(None, 'head'), may hold values from -0.109375 to 0.109375
- rate_weight: bfloat16 [2, 32, 3072], P(None, 'head'), may hold values from -0.109375 to 0.109375
- first_init: float32 [2, 32, 64, 256], P(None, 'head'), may hold values from -0.75 to 0.75
- first_bias: float32 [2, 32, 256], P(None, 'head'), may hold values from -3 to 3
- second_init: float32 [2, 32, 256, 64], P(None, 'head'), may hold values from -0.375 to 0.375
- second_bias: float32 [2, 32, 64], P(None, 'head'), may hold values from -3 to 3
- norm_gain: float32 [2, 32, 64], P(None, 'head'), may hold values from 0.25 to 1.75
- norm_bias: float32 [2, 32, 64], P(None, 'head'), may hold values from -3 to 3
- out_weight: bfloat16 [2, 2048, 3072], P(None, 'head'), may hold values from -0.125 to 0.125
Outputs:
- result: bfloat16 [4, 2048, 3072], P(None, ('seq', 'head'))
The draws below stay inside these ranges and needn't reach their ends.
All inputs are finite; a program needn't handle non-finite values.
Results may differ from the reference program's by a relative error of at most 0.008.
Values may be sent and summed in bfloat16 or wider, within the bound.
A program may use at most 128 MiB of HBM per device.

```python
import jax
import jax.numpy as jnp
from jax import lax

D = 3072
HEAD_SIZE = 64
INNER = 256
MINI = 64
LAYERS = 2
SEQS = 4
HEADS = 32
LEN = 2048


def level_of(own_key, shape, cuts, least, high):
    level = 1.0
    for axis_at, blocks in cuts:
        steps = jax.random.uniform(jax.random.fold_in(jax.random.fold_in(own_key, 6), axis_at), (blocks,), jnp.float32, least / len(cuts), high / len(cuts))
        level = level * jnp.repeat(jnp.exp(steps), shape[axis_at] // blocks).reshape((-1,) + (1,) * (len(shape) - 1 - axis_at))
    return level


def normal_values(stream_key, dims, spread, bound, shards=(), dtype=jnp.bfloat16):
    factor_of = level_of(stream_key, dims, shards, -0.22, 0.18) if shards else 1.0
    drawn = jax.random.normal(stream_key, dims, jnp.float32) * spread * factor_of
    return jnp.minimum(jnp.maximum(drawn, -bound), bound).astype(dtype)


def setup_inputs(seed: int = 0) -> dict:
    arg_keys = jax.random.split(jax.random.key(seed), 11)
    return {
        "tokens": normal_values(arg_keys[0], (SEQS, LEN, D), 1.0, 6.0, ((1, 256),)),
        "qkv_weight": normal_values(arg_keys[1], (LAYERS, HEADS, 3 * HEAD_SIZE, D), D ** -0.5, 0.109375, ((1, 32),)),
        "rate_weight": normal_values(arg_keys[2], (LAYERS, HEADS, D), D ** -0.5, 0.109375, ((1, 32),)),
        "first_init": normal_values(arg_keys[3], (LAYERS, HEADS, HEAD_SIZE, INNER), HEAD_SIZE ** -0.5, 0.75, ((1, 32),), jnp.float32),
        "first_bias": normal_values(arg_keys[4], (LAYERS, HEADS, INNER), 0.5, 3.0, ((1, 32),), jnp.float32),
        "second_init": normal_values(arg_keys[5], (LAYERS, HEADS, INNER, HEAD_SIZE), INNER ** -0.5, 0.375, ((1, 32),), jnp.float32),
        "second_bias": normal_values(arg_keys[6], (LAYERS, HEADS, HEAD_SIZE), 0.5, 3.0, ((1, 32),), jnp.float32),
        "norm_gain": jnp.clip(1.0 + 0.15 * jax.random.normal(arg_keys[7], (LAYERS, HEADS, HEAD_SIZE), jnp.float32), 0.25, 1.75),
        "norm_bias": normal_values(arg_keys[8], (LAYERS, HEADS, HEAD_SIZE), 0.5, 3.0, ((1, 32),), jnp.float32),
        "out_weight": normal_values(arg_keys[9], (LAYERS, HEADS * HEAD_SIZE, D), (HEADS * HEAD_SIZE) ** -0.5, 0.125, ((1, 32),)),
    }


eps = 1e-06

def gelu_pair(z):
    coef = 0.7978845608028654
    inner = coef * (z + 0.044715 * z * z * z)
    tanh_val = jnp.tanh(inner)
    value = 0.5 * z * (1.0 + tanh_val)
    slope = 0.5 * (1.0 + tanh_val) + 0.5 * z * (1.0 - tanh_val * tanh_val) * coef * (1.0 + 3.0 * 0.044715 * z * z)
    return (value, slope)

def norm_parts(z, gain, shift):
    center = z - lax.optimization_barrier(jnp.mean(z, axis=-1, keepdims=True))
    inverse = lax.rsqrt(lax.optimization_barrier(jnp.mean(center * center, axis=-1, keepdims=True)) + eps)
    normed = center * inverse
    return (normed, inverse, gain * normed + shift)

def mini_step(state, batch, gain, shift):
    w_first, b_first, w_second, b_second = state
    queries, keys, values, rates = batch
    high = lax.Precision.HIGHEST

    def matmul(left, right):
        return jnp.dot(left, right, precision=high)
    z_one = matmul(keys, w_first) + b_first
    act_one, slope = gelu_pair(z_one)
    z_two = matmul(act_one, w_second) + b_second
    normed, inverse, recon = norm_parts(z_two, gain, shift)
    grad_hat = (recon - (values - keys)) * gain
    width = z_two.shape[-1]
    grad_two = inverse / width * (width * grad_hat - lax.optimization_barrier(jnp.sum(grad_hat, axis=-1, keepdims=True)) - normed * lax.optimization_barrier(jnp.sum(grad_hat * normed, axis=-1, keepdims=True)))
    grad_one = matmul(grad_two, w_second.T) * slope
    count = queries.shape[0]
    lower = (lax.broadcasted_iota(jnp.int32, (count, count), 0) >= lax.broadcasted_iota(jnp.int32, (count, count), 1)).astype(jnp.float32)
    weights = lower * rates[None, :]
    z_bar = matmul(queries, w_first) + b_first - matmul(weights * matmul(queries, keys.T), grad_one) - matmul(weights, grad_one)
    act_bar, unused = gelu_pair(z_bar)
    z_bar_two = matmul(act_bar, w_second) + b_second - matmul(weights * matmul(act_bar, act_one.T), grad_two) - matmul(weights, grad_two)
    unused_a, unused_b, final = norm_parts(z_bar_two, gain, shift)
    output = queries + final
    new_first = w_first - matmul((keys * rates[:, None]).T, grad_one)
    new_bfirst = b_first - matmul(rates[None, :], grad_one)[0]
    new_second = w_second - matmul((act_one * rates[:, None]).T, grad_two)
    new_bsecond = b_second - matmul(rates[None, :], grad_two)[0]
    return ((new_first, new_bfirst, new_second, new_bsecond), output)

def ttt_run(state, queries, keys, values, rates, gain, shift):
    length, size = queries.shape
    blocks = length // MINI
    batches = (queries.reshape(blocks, MINI, size), keys.reshape(blocks, MINI, size), values.reshape(blocks, MINI, size), rates.reshape(blocks, MINI))
    final, outputs = lax.scan(lambda carry, batch: mini_step(carry, batch, gain, shift), state, batches)
    return (final, outputs.reshape(length, size))

def layer(inputs, qkv_w, rate_w, w_first, b_first, w_second, b_second, gain, shift, out_w, reverse):
    source = jnp.flip(inputs, 1) if reverse else inputs
    floats = source.astype(jnp.float32)
    mixed = jnp.einsum('bld,hed->bhle', floats, qkv_w.astype(jnp.float32))
    logits = jnp.einsum('bld,hd->bhl', floats, rate_w.astype(jnp.float32))
    rates = jax.nn.sigmoid(logits) / HEAD_SIZE
    queries = mixed[..., :HEAD_SIZE]
    keys = mixed[..., HEAD_SIZE:2 * HEAD_SIZE]
    values = mixed[..., 2 * HEAD_SIZE:]

    def one_head(state, q, k, v, r, g, s):
        return ttt_run(state, q, k, v, r, g, s)[1]
    per_head = jax.vmap(one_head, in_axes=(0, 0, 0, 0, 0, 0, 0))
    per_seq = jax.vmap(per_head, in_axes=(None, 0, 0, 0, 0, None, None))
    outs = per_seq((w_first, b_first, w_second, b_second), queries, keys, values, rates, gain, shift)
    joined = jnp.transpose(outs, (0, 2, 1, 3)).reshape(outs.shape[0], outs.shape[2], outs.shape[1] * outs.shape[3])
    if reverse:
        joined = jnp.flip(joined, 1)
    joined = joined.astype(jnp.bfloat16)
    partial_sum = jnp.einsum('ble,ed->bld', joined.astype(jnp.float32), out_w.astype(jnp.float32))
    return (inputs.astype(jnp.float32) + partial_sum).astype(jnp.bfloat16)

def reference(tokens, qkv_weight, rate_weight, first_init, first_bias, second_init, second_bias, norm_gain, norm_bias, out_weight):
    middle = layer(tokens, qkv_weight[0], rate_weight[0], first_init[0], first_bias[0], second_init[0], second_bias[0], norm_gain[0], norm_bias[0], out_weight[0], False)
    return layer(middle, qkv_weight[1], rate_weight[1], first_init[1], first_bias[1], second_init[1], second_bias[1], norm_gain[1], norm_bias[1], out_weight[1], True)
```

```python
import functools

import jax
import jax.numpy as jnp
from jax import lax
from jax.experimental import pallas as pl
from jax.experimental.pallas import tpu as pltpu
from jax.sharding import PartitionSpec as P

HEAD_SIZE = 64
MINI = 64
EPS = 1e-06
BF = jnp.bfloat16
F32 = jnp.float32


def dot(a, b, dims):
    return lax.dot_general(a, b, (dims, ((), ())), preferred_element_type=F32)


NN = ((1,), (0,))
NT = ((1,), (1,))
TN = ((0,), (0,))


def gelu_pair(z):
    coef = 0.7978845608028654
    zz = z * z
    cube = 0.044715 * coef * zz
    tanh_val = jnp.tanh(z * (coef + cube))
    half = 0.5 + 0.5 * tanh_val
    value = z * half
    slope = half + value * (1.0 - tanh_val) * (coef + 3.0 * cube)
    return value, slope


def split(x):
    high = x.astype(BF)
    return high, (x - high.astype(F32)).astype(BF)


def scan_kernel(
    forward,
    s_ref,
    d_ref,
    r_ref,
    w1_ref,
    b1_ref,
    w2_ref,
    b2_ref,
    g_ref,
    c_ref,
    o_ref,
    w1d,
    b1,
    w2t,
    w2d,
    b2,
    g1h_p,
    g1l_p,
    g2h_p,
    g2l_p,
    th_p,
    tl_p,
    sh_p,
    sl_p,
):
    steps, size, lanes = s_ref.shape
    hidden = w1_ref.shape[1]
    half = lanes // 2
    w1d[...] = jnp.concatenate([w1_ref[...], w1_ref[...]], 0).T
    b1[...] = jnp.broadcast_to(b1_ref[...], (lanes, hidden)).T
    centred = w2_ref[...] - jnp.mean(w2_ref[...], axis=1, keepdims=True)
    w2d[...] = jnp.concatenate([centred, centred], 1)
    w2t[...] = centred.T
    b2[...] = jnp.broadcast_to(b2_ref[...] - jnp.mean(b2_ref[...]), (size, lanes))
    for ref in (g1h_p, g1l_p, g2h_p, g2l_p, th_p, tl_p, sh_p, sl_p):
        ref[...] = jnp.zeros_like(ref)

    row = lax.broadcasted_iota(jnp.int32, (lanes, lanes), 0) - half
    col = lax.broadcasted_iota(jnp.int32, (lanes, lanes), 1)
    seen = (row <= col) if forward else (row >= col)
    first_mask = (seen | (col >= half)).astype(F32)
    second_mask = (~seen & (col < half)).astype(F32)
    low_half = lax.broadcasted_iota(jnp.int32, (hidden, lanes), 1) < half
    gain = jnp.broadcast_to(g_ref[...], (size, lanes))
    shift = jnp.broadcast_to(c_ref[...], (size, lanes))
    gain2 = gain * gain
    ones = jnp.ones((lanes, lanes), BF)
    zeros = jnp.zeros((lanes, lanes), BF)
    blank = jnp.zeros((half, lanes), BF)

    def stacked(doubled):
        high = doubled.astype(BF)
        low = (doubled - high.astype(F32)).astype(BF)
        return jnp.concatenate([jnp.where(low_half, high, low), high], 1)

    def step(j, carry):
        s = s_ref[j]
        sh, sl = split(s)
        shp, slp = sh_p[...], sl_p[...]
        g1h, g1l = g1h_p[...], g1l_p[...]
        g2h, g2l = g2h_p[...], g2l_p[...]
        thp, tlp = th_p[...], tl_p[...]
        g1s = jnp.concatenate([g1h, g1l, g1h], 1)
        g2s = jnp.concatenate([g2h, g2l, g2h], 1)
        w1_old, b1_old = w1d[...], b1[...]
        w2t_new = w2t[...] - dot(g2s, jnp.concatenate([thp, thp, tlp], 1), NT)
        g2dh = jnp.concatenate([g2h, g2h], 0)
        g2dl = jnp.concatenate([g2l, g2l], 0)
        w2d_new = w2d[...] - dot(
            jnp.concatenate([thp, tlp, thp], 1), jnp.concatenate([g2dh, g2dh, g2dl], 1), NT
        )
        b2_new = b2[...] - jnp.sum(g2h.astype(F32) + g2l.astype(F32), axis=1, keepdims=True)
        w2t[...] = w2t_new
        w2d[...] = w2d_new
        b2[...] = b2_new
        sd_high = jnp.concatenate([shp, shp, ones], 0)
        sd_low = jnp.concatenate([slp, slp, zeros], 0)
        change = dot(g1s, jnp.concatenate([sd_high, sd_high, sd_low], 1), NT)
        w1d[...] = w1_old - change[:, :lanes]
        b1[...] = b1_old - change[:, lanes:]
        pair = dot(
            jnp.concatenate([shp, slp, shp], 0), jnp.concatenate([sh, sh, sl], 0), TN
        )
        ph, pl_ = split((pair + 1.0) * first_mask)
        z = (
            dot(stacked(w1_old), jnp.concatenate([sh, sh, sl, blank], 0), NN)
            + b1_old
            - dot(g1s, jnp.concatenate([ph, ph, pl_], 0), NN)
        )
        value, slope = gelu_pair(z)
        th, tl = split(value)
        w2h, w2l = split(w2t_new)
        z2 = (
            dot(
                jnp.concatenate([w2h, w2l, w2h], 1), jnp.concatenate([th, th, tl], 0), NN
            )
            + b2_new
        )
        cross = dot(
            jnp.concatenate([thp, tlp, thp], 0), jnp.concatenate([th, th, tl], 0), TN
        )
        ch, cl = split((cross + 1.0) * second_mask)
        z2o = z2 + dot(g2s, jnp.concatenate([ch, ch, cl], 0), NN)
        d0 = gain * (shift - d_ref[j])
        zz = z2 * z2
        s_zz = jnp.sum(zz, axis=0, keepdims=True)
        s_g = jnp.sum(gain2 * z2, axis=0, keepdims=True)
        s_gzz = jnp.sum(gain2 * zz, axis=0, keepdims=True)
        s_dz = jnp.sum(d0 * z2, axis=0, keepdims=True)
        s_d = jnp.sum(d0, axis=0, keepdims=True)
        inv = lax.rsqrt(s_zz * (1.0 / size) + EPS)
        sum_h = inv * s_g + s_d
        sum_hn = inv * (inv * s_gzz + s_dz)
        n = z2 * inv
        scale = inv * r_ref[j]
        g2h_n, g2l_n = split(scale * (gain2 * n + d0 - (sum_h + n * sum_hn) * (1.0 / size)))
        g1 = (
            dot(stacked(w2d_new), jnp.concatenate([g2h_n, g2h_n, g2l_n, blank], 0), NN) * slope
        )
        g1h_n, g1l_n = split(g1)
        s_oo = jnp.sum(z2o * z2o, axis=0, keepdims=True)
        no = z2o * lax.rsqrt(s_oo * (1.0 / size) + EPS)
        o_ref[j] = (s + gain * no + shift).astype(BF)
        g1h_p[...] = g1h_n
        g1l_p[...] = g1l_n
        g2h_p[...] = g2h_n
        g2l_p[...] = g2l_n
        th_p[...] = th
        tl_p[...] = tl
        sh_p[...] = sh
        sl_p[...] = sl
        return carry

    lax.fori_loop(0, steps, step, 0)


def run_scan(forward, s, d, r, w1, b1, w2, b2, g, c):
    steps, size, lanes = s.shape
    hidden = w1.shape[1]
    vmem = pl.BlockSpec(memory_space=pltpu.VMEM)
    pair = lambda shape: [pltpu.VMEM(shape, BF)] * 2
    return pl.pallas_call(
        functools.partial(scan_kernel, forward),
        out_shape=jax.ShapeDtypeStruct((steps, size, lanes), BF),
        in_specs=[vmem] * 9,
        out_specs=vmem,
        scratch_shapes=[
            pltpu.VMEM((hidden, lanes), F32),
            pltpu.VMEM((hidden, lanes), F32),
            pltpu.VMEM((size, hidden), F32),
            pltpu.VMEM((hidden, lanes), F32),
            pltpu.VMEM((size, lanes), F32),
            *pair((hidden, lanes)),
            *pair((size, lanes)),
            *pair((hidden, lanes)),
            *pair((size, lanes)),
        ],
        compiler_params=pltpu.CompilerParams(vmem_limit_bytes=32 * 2**20),
        cost_estimate=pl.CostEstimate(
            flops=steps * 2 * 3008 * 65536, bytes_accessed=5 * steps * size * lanes * 2, transcendentals=0
        ),
        name="scan_fwd" if forward else "scan_rev",
    )(s, d, r, w1, b1, w2, b2, g, c)


def assemble(chain, forward):
    shards, rows, tokens = chain.shape
    n = shards * tokens // MINI
    blocks = chain.reshape(shards, rows, tokens // MINI, MINI).transpose(0, 2, 1, 3).reshape(n, rows, MINI)
    if not forward:
        blocks = blocks[::-1]
    q = blocks[:, :HEAD_SIZE]
    k = blocks[:, HEAD_SIZE : 2 * HEAD_SIZE]
    v = blocks[:, 2 * HEAD_SIZE : 3 * HEAD_SIZE]
    logit = blocks[:, 3 * HEAD_SIZE : 3 * HEAD_SIZE + 1]
    before = lambda x: jnp.pad(x, ((1, 0), (0, 0), (0, 0)))
    after = lambda x: jnp.pad(x, ((0, 1), (0, 0), (0, 0)))
    s = jnp.concatenate([before(q), after(k)], -1)
    d = jnp.pad(v - k, ((0, 1), (0, 0), (MINI, 0)))
    r = jnp.pad(jax.nn.sigmoid(logit) / HEAD_SIZE, ((0, 1), (0, 0), (MINI, 0)))
    return s, d, r


def chain_heads(mixed, forward, params):
    seqs = mixed.shape[0]
    shards = lax.axis_size("seq")
    copies = shards // seqs
    send = jnp.repeat(mixed, copies, axis=0)
    chain = lax.all_to_all(send, "seq", 0, 0, tiled=True)
    out = run_scan(forward, *assemble(chain, forward), *params)
    o = out[1:, :, :MINI]
    if not forward:
        o = o[::-1]
    n = o.shape[0]
    part = n // shards // copies
    o = o.reshape(shards, copies, part, HEAD_SIZE, MINI)
    mine = lax.dynamic_index_in_dim(o, lax.rem(lax.axis_index("seq"), copies), 1, keepdims=False)
    return mine


def back_to_shards(mine, seqs):
    shards, part, size, mini = mine.shape
    back = lax.all_to_all(mine, "seq", 0, 0, tiled=True)
    return back.reshape(seqs, shards // seqs * part, size, mini)


def body(
    tokens,
    qkv_weight,
    rate_weight,
    first_init,
    first_bias,
    second_init,
    second_bias,
    norm_gain,
    norm_bias,
    out_weight,
):
    seqs, rows_here, width = tokens.shape
    shards = lax.axis_size("seq")
    heads = lax.axis_size("head")
    index = lax.axis_index("seq")
    cut = width // shards

    def weights(layer):
        return jnp.concatenate(
            [qkv_weight[layer, 0], rate_weight[layer], jnp.zeros((7, width), BF)], 0
        )

    def params(layer):
        return (
            first_init[layer, 0],
            first_bias[layer],
            second_init[layer, 0],
            second_bias[layer].T,
            norm_gain[layer].T,
            norm_bias[layer].T,
        )

    def out_slice(layer):
        piece = lax.dynamic_slice_in_dim(out_weight[layer], index * cut, cut, 1)
        return lax.all_gather(piece, "head", axis=0, tiled=True)

    def project(layer, full):
        return jnp.einsum("ed,bld->bel", weights(layer), full, preferred_element_type=F32)

    def own_rows(o):
        split = o.reshape(seqs, -1, HEAD_SIZE, MINI // rows_here, rows_here)
        split = split.transpose(1, 3, 0, 4, 2).reshape(heads, seqs * rows_here, HEAD_SIZE)
        got = lax.all_to_all(split, "head", 0, 0, tiled=True)
        mine = got.transpose(1, 0, 2).reshape(seqs * rows_here, heads * HEAD_SIZE)
        return lax.all_gather(mine, "seq", axis=0, tiled=True)

    def layer_out(layer, local, o, sliced):
        delta = jnp.dot(own_rows(o), sliced, preferred_element_type=F32)
        delta = delta.reshape(shards, seqs * rows_here, cut)
        delta = lax.all_to_all(delta, "seq", 0, 0, tiled=True)
        delta = delta.transpose(1, 0, 2).reshape(seqs, rows_here, width)
        return (local.astype(F32) + delta).astype(BF)

    full = lax.all_gather(tokens, "head", axis=1, tiled=True)
    mixed = project(0, full)
    sliced = out_slice(0), out_slice(1)
    o = back_to_shards(chain_heads(mixed, True, params(0)), seqs)
    middle = layer_out(0, tokens, o, sliced[0])
    full = lax.all_gather(middle, "head", axis=1, tiled=True)
    o = back_to_shards(chain_heads(project(1, full), False, params(1)), seqs)
    return layer_out(1, middle, o, sliced[1])


def solution(mesh):
    placed = (
        P(None, ("seq", "head"), None),
        P(None, "head", None, None),
        P(None, "head", None),
        P(None, "head", None, None),
        P(None, "head", None),
        P(None, "head", None, None),
        P(None, "head", None),
        P(None, "head", None),
        P(None, "head", None),
        P(None, "head", None),
    )
    return jax.shard_map(
        body, mesh=mesh, in_specs=placed, out_specs=P(None, ("seq", "head"), None), check_vma=False
    )
```

```python
import functools

import jax
import jax.numpy as jnp
from jax import lax
from jax.experimental import pallas as pl
from jax.experimental.pallas import tpu as pltpu
from jax.sharding import PartitionSpec as P

HEAD_SIZE = 64
MINI = 64
EPS = 1e-06
BF = jnp.bfloat16
F32 = jnp.float32


def dot(a, b, dims):
    return lax.dot_general(a, b, (dims, ((), ())), preferred_element_type=F32)


NN = ((1,), (0,))
NT = ((1,), (1,))
TN = ((0,), (0,))


def gelu_pair(z):
    coef = 0.7978845608028654
    zz = z * z
    cube = 0.044715 * coef * zz
    tanh_val = jnp.tanh(z * (coef + cube))
    half = 0.5 + 0.5 * tanh_val
    value = z * half
    slope = half + value * (1.0 - tanh_val) * (coef + 3.0 * cube)
    return value, slope


def split(x):
    high = x.astype(BF)
    return high, (x - high.astype(F32)).astype(BF)


def pick_barrier(peers):
    barrier = pltpu.get_barrier_semaphore()
    for axis, count in peers:
        here = lax.axis_index(axis)

        def greet(t, carry):
            pl.semaphore_signal(
                barrier,
                inc=1,
                device_id={axis: lax.rem(here + t, count)},
                device_id_type=pl.DeviceIdType.MESH,
            )
            return carry

        lax.fori_loop(1, count, greet, 0)
    pl.semaphore_wait(barrier, sum(count - 1 for _, count in peers))


def remote(src, dst, send_sem, recv_sem, where):
    return pltpu.make_async_remote_copy(
        src_ref=src,
        dst_ref=dst,
        send_sem=send_sem,
        recv_sem=recv_sem,
        device_id=where,
        device_id_type=pl.DeviceIdType.MESH,
    )


def scan_kernel(
    forward,
    shards,
    mixed_ref,
    w1_ref,
    b1_ref,
    w2_ref,
    b2_ref,
    g_ref,
    c_ref,
    o_ref,
    chain,
    outs,
    send_sem,
    recv_sem,
    w1d,
    b1,
    w2t,
    w2d,
    b2,
    g1h_p,
    g1l_p,
    g2h_p,
    g2l_p,
    th_p,
    tl_p,
    sh_p,
    sl_p,
):
    size, hidden = w1_ref.shape
    lanes = 2 * MINI
    half = MINI
    parts, seqs, per, _ = mixed_ref.shape
    copies = shards // seqs
    per = half // per
    minis = parts // per
    steps = shards * minis + 1
    index = lax.axis_index("seq")
    lane = lax.rem(lax.axis_index("head"), copies)
    row_here = lax.div(index, copies)
    active = lax.rem(index, copies) == lane

    pick_barrier([("seq", shards)])
    landing = chain.at[pl.ds(index * parts, parts)]
    sends = []
    for t in range(1, seqs):
        there = lax.rem(row_here + t, seqs)
        sends.append(
            remote(
                mixed_ref.at[:, there],
                landing,
                send_sem.at[t],
                recv_sem.at[index],
                {"seq": there * copies + lane},
            )
        )
    own = pltpu.make_async_copy(mixed_ref.at[:, row_here], landing, recv_sem.at[index])
    across = remote(
        mixed_ref.at[:, row_here],
        landing,
        send_sem.at[0],
        recv_sem.at[index],
        {"seq": row_here * copies + 1 - lax.rem(index, copies)},
    )

    @pl.when(active)
    def _():
        own.start()

    @pl.when(jnp.logical_not(active))
    def _():
        across.start()

    for copy in sends:
        copy.start()

    def place(j):
        j = jnp.clip(j, 0, steps - 2)
        return j if forward else steps - 2 - j

    def wait_for(shard):
        pltpu.make_async_copy(
            mixed_ref.at[:, row_here], chain.at[pl.ds(shard * parts, parts)], recv_sem.at[shard]
        ).wait()

    w1d[...] = jnp.concatenate([w1_ref[...], w1_ref[...]], 0).T
    b1[...] = jnp.broadcast_to(b1_ref[...], (lanes, hidden)).T
    centred = w2_ref[...] - jnp.mean(w2_ref[...], axis=1, keepdims=True)
    w2d[...] = jnp.concatenate([centred, centred], 1)
    w2t[...] = centred.T
    b2[...] = jnp.broadcast_to(b2_ref[...] - jnp.mean(b2_ref[...]), (size, lanes))
    for ref in (g1h_p, g1l_p, g2h_p, g2l_p, th_p, tl_p, sh_p, sl_p):
        ref[...] = jnp.zeros_like(ref)

    row = lax.broadcasted_iota(jnp.int32, (lanes, lanes), 0) - half
    col = lax.broadcasted_iota(jnp.int32, (lanes, lanes), 1)
    seen = (row <= col) if forward else (row >= col)
    first_mask = (seen | (col >= half)).astype(F32)
    second_mask = (~seen & (col < half)).astype(F32)
    left = col[:size] < half
    low_half = lax.broadcasted_iota(jnp.int32, (hidden, lanes), 1) < half
    gain = jnp.broadcast_to(g_ref[...], (size, lanes))
    shift = jnp.broadcast_to(c_ref[...], (size, lanes))
    gain2 = gain * gain
    ones = jnp.ones((lanes, lanes), BF)
    zeros = jnp.zeros((lanes, lanes), BF)
    blank = jnp.zeros((half, lanes), BF)

    def stacked(doubled):
        high = doubled.astype(BF)
        low = (doubled - high.astype(F32)).astype(BF)
        return jnp.concatenate([jnp.where(low_half, high, low), high], 1)

    def step(j, carry):
        @pl.when((lax.rem(j, minis) == 0) & (j < steps - 1))
        def _():
            arrived = lax.div(place(j), minis)
            wait_for(arrived)

        before, now = place(j - 1), place(j)
        old = chain[pl.ds(before * per, per)].reshape(half, 4 * size)
        new = chain[pl.ds(now * per, per)].reshape(half, 4 * size)
        turned = jnp.concatenate([old[:, :lanes], new[:, :lanes]], 0).T
        s = jnp.where(left, turned[:size], turned[size:])
        turned = jnp.concatenate([old[:, lanes:], new[:, lanes:]], 0).T
        target = turned[:size] - s
        rate = jnp.where(
            left[:1], 0.0, jax.nn.sigmoid(turned[size : size + 1]) * (1.0 / HEAD_SIZE)
        )
        sh, sl = split(s)
        shp, slp = sh_p[...], sl_p[...]
        g1h, g1l = g1h_p[...], g1l_p[...]
        g2h, g2l = g2h_p[...], g2l_p[...]
        thp, tlp = th_p[...], tl_p[...]
        g1s = jnp.concatenate([g1h, g1l, g1h], 1)
        g2s = jnp.concatenate([g2h, g2l, g2h], 1)
        w1_old, b1_old = w1d[...], b1[...]
        w2t_new = w2t[...] - dot(g2s, jnp.concatenate([thp, thp, tlp], 1), NT)
        g2dh = jnp.concatenate([g2h, g2h], 0)
        g2dl = jnp.concatenate([g2l, g2l], 0)
        w2d_new = w2d[...] - dot(
            jnp.concatenate([thp, tlp, thp], 1), jnp.concatenate([g2dh, g2dh, g2dl], 1), NT
        )
        b2_new = b2[...] - jnp.sum(g2h.astype(F32) + g2l.astype(F32), axis=1, keepdims=True)
        w2t[...] = w2t_new
        w2d[...] = w2d_new
        b2[...] = b2_new
        sd_high = jnp.concatenate([shp, shp, ones], 0)
        sd_low = jnp.concatenate([slp, slp, zeros], 0)
        change = dot(g1s, jnp.concatenate([sd_high, sd_high, sd_low], 1), NT)
        w1d[...] = w1_old - change[:, :lanes]
        b1[...] = b1_old - change[:, lanes:]
        pair = dot(
            jnp.concatenate([shp, slp, shp], 0), jnp.concatenate([sh, sh, sl], 0), TN
        )
        ph, pl_ = split((pair + 1.0) * first_mask)
        z = (
            dot(stacked(w1_old), jnp.concatenate([sh, sh, sl, blank], 0), NN)
            + b1_old
            - dot(g1s, jnp.concatenate([ph, ph, pl_], 0), NN)
        )
        value, slope = gelu_pair(z)
        th, tl = split(value)
        w2h, w2l = split(w2t_new)
        z2 = (
            dot(
                jnp.concatenate([w2h, w2l, w2h], 1), jnp.concatenate([th, th, tl], 0), NN
            )
            + b2_new
        )
        cross = dot(
            jnp.concatenate([thp, tlp, thp], 0), jnp.concatenate([th, th, tl], 0), TN
        )
        ch, cl = split((cross + 1.0) * second_mask)
        z2o = z2 + dot(g2s, jnp.concatenate([ch, ch, cl], 0), NN)
        d0 = gain * (shift - target)
        zz = z2 * z2
        s_zz = jnp.sum(zz, axis=0, keepdims=True)
        s_g = jnp.sum(gain2 * z2, axis=0, keepdims=True)
        s_gzz = jnp.sum(gain2 * zz, axis=0, keepdims=True)
        s_dz = jnp.sum(d0 * z2, axis=0, keepdims=True)
        s_d = jnp.sum(d0, axis=0, keepdims=True)
        inv = lax.rsqrt(s_zz * (1.0 / size) + EPS)
        sum_h = inv * s_g + s_d
        sum_hn = inv * (inv * s_gzz + s_dz)
        n = z2 * inv
        scale = inv * rate
        g2h_n, g2l_n = split(scale * (gain2 * n + d0 - (sum_h + n * sum_hn) * (1.0 / size)))
        g1 = (
            dot(stacked(w2d_new), jnp.concatenate([g2h_n, g2h_n, g2l_n, blank], 0), NN) * slope
        )
        g1h_n, g1l_n = split(g1)
        s_oo = jnp.sum(z2o * z2o, axis=0, keepdims=True)
        no = z2o * lax.rsqrt(s_oo * (1.0 / size) + EPS)
        done = (s + gain * no + shift).T[:half].reshape(per, half // per, size)
        outs[pl.ds(lax.rem(before, minis) * per, per), lax.div(before, minis)] = done
        g1h_p[...] = g1h_n
        g1l_p[...] = g1l_n
        g2h_p[...] = g2h_n
        g2l_p[...] = g2l_n
        th_p[...] = th
        tl_p[...] = tl
        sh_p[...] = sh
        sl_p[...] = sl
        return carry

    @pl.when(active)
    def _():
        lax.fori_loop(0, steps, step, 0)
        o_ref[...] = outs[...].reshape(o_ref.shape).astype(BF)

    @pl.when(jnp.logical_not(active))
    def _():
        across.wait_send()

    for copy in sends:
        copy.wait_send()


def run_scan(forward, number, mixed, w1, b1, w2, b2, g, c):
    parts, seqs, rows, width = mixed.shape
    shards = lax.axis_size("seq")
    size, hidden = w1.shape
    lanes = 2 * MINI
    vmem = pl.BlockSpec(memory_space=pltpu.VMEM)
    pair = lambda shape: [pltpu.VMEM(shape, BF)] * 2
    return pl.pallas_call(
        functools.partial(scan_kernel, forward, shards),
        out_shape=jax.ShapeDtypeStruct((parts, shards * rows, size), BF),
        in_specs=[pl.BlockSpec(memory_space=pl.ANY)] + [vmem] * 6,
        out_specs=vmem,
        scratch_shapes=[
            pltpu.VMEM((shards * parts, rows, width), F32),
            pltpu.VMEM((parts, shards, rows, size), F32),
            pltpu.SemaphoreType.DMA((seqs,)),
            pltpu.SemaphoreType.DMA((shards,)),
            pltpu.VMEM((hidden, lanes), F32),
            pltpu.VMEM((hidden, lanes), F32),
            pltpu.VMEM((size, hidden), F32),
            pltpu.VMEM((hidden, lanes), F32),
            pltpu.VMEM((size, lanes), F32),
            *pair((hidden, lanes)),
            *pair((size, lanes)),
            *pair((hidden, lanes)),
            *pair((size, lanes)),
        ],
        compiler_params=pltpu.CompilerParams(
            vmem_limit_bytes=40 * 2**20, collective_id=number, has_side_effects=True
        ),
        cost_estimate=pl.CostEstimate(
            flops=33 * 2 * 3008 * 65536, bytes_accessed=2 * 2**20, transcendentals=0
        ),
        name="scan_fwd" if forward else "scan_rev",
    )(mixed, w1, b1, w2, b2, g, c)


def gather_blocks(local, full, own_sem, send_sem, recv_sem):
    heads = full.shape[0]
    ring = heads // 4
    head = lax.axis_index("head")
    x = lax.div(head, 2 * ring)
    z = lax.rem(lax.div(head, 2), ring)
    core = lax.rem(head, 2)
    name = lambda x_, z_, c_: x_ * 2 * ring + lax.rem(z_ + 2 * ring, ring) * 2 + c_
    up, down = name(x, z + 1, core), name(x, z - 1, core)
    beside, twin = name(1 - x, z, core), name(x, z, 1 - core)
    started = []

    def send(block, part, kind, to, src=None):
        dst = full.at[block, part]
        copy = remote(
            dst if src is None else src,
            dst,
            send_sem.at[kind, block, part],
            recv_sem.at[block, part],
            {"head": to},
        )
        copy.start()
        started.append(copy)

    def arrive(block, part):
        pltpu.make_async_copy(
            local.at[part], full.at[block, part], recv_sem.at[block, part]
        ).wait()

    own = pltpu.make_async_copy(local, full.at[head], own_sem)
    own.start()
    for kind, part, to in (
        (2, 1, beside),
        (0, 0, up),
        (1, 0, down),
        (0, 1, up),
        (1, 1, down),
        (2, 0, beside),
        (3, 0, twin),
        (3, 1, twin),
    ):
        send(head, part, kind, to, local.at[part])
    other = name(1 - x, z, core)
    arrive(other, 1)
    send(other, 1, 0, up)
    send(other, 1, 1, down)
    send(other, 1, 3, twin)
    last = ring // 2
    turn = 1 - 2 * core
    for k in range(1, last + 1):
        ways = ((1, up, 0), (-1, down, 1)) if k < last else ((turn, None, 0),)
        for sign, to, kind in ways:
            mine, others = name(x, z - sign * k, core), name(1 - x, z - sign * k, core)
            for block, part in ((mine, 0), (mine, 1), (others, 1)):
                arrive(block, part)
                if k < last - 1:
                    send(block, part, kind, to)
                if part == 0:
                    send(block, 0, 2, beside)
                send(block, part, 3, twin)
        if k == last - 1:
            to = name(x, z + turn, core)
            mine, others = name(x, z - turn * k, core), name(1 - x, z - turn * k, core)
            for block, part in ((mine, 0), (mine, 1), (others, 1)):
                send(block, part, 0, to)
        crossed = (0, k, -k) if k == 1 else ((k, -k) if k < last else (k,))
        for off in crossed:
            block = name(1 - x, z + off, core)
            arrive(block, 0)
            send(block, 0, 3, twin)

    def from_twin(t, carry):
        block = 2 * t + 1 - core
        arrive(block, 0)
        arrive(block, 1)
        return carry

    lax.fori_loop(0, heads // 2, from_twin, 0)
    own.wait()
    for copy in started:
        copy.wait_send()


def gather_sems(heads):
    return [
        pltpu.SemaphoreType.DMA,
        pltpu.SemaphoreType.DMA((4, heads, 2)),
        pltpu.SemaphoreType.DMA((heads, 2)),
    ]


def gather_kernel(heads, local, full, own_sem, send_sem, recv_sem):
    pick_barrier([("head", heads)])
    gather_blocks(local, full, own_sem, send_sem, recv_sem)


def run_gather(local, number):
    heads = lax.axis_size("head")
    anyspec = pl.BlockSpec(memory_space=pl.ANY)
    return pl.pallas_call(
        functools.partial(gather_kernel, heads),
        out_shape=jax.ShapeDtypeStruct((heads, *local.shape), BF),
        in_specs=[anyspec],
        out_specs=anyspec,
        scratch_shapes=gather_sems(heads),
        compiler_params=pltpu.CompilerParams(collective_id=number, has_side_effects=True),
        name="gather_tokens",
    )(local)


def out_kernel(
    heads,
    shards,
    seqs,
    gathers,
    o_ref,
    w_ref,
    local_ref,
    *rest,
):
    result, rest = rest[0], rest[1:]
    full = None
    if gathers:
        full, rest = rest[0], rest[1:]
    blocks, joined, delta, parts, sem_a, sem_b, sem_c, sem_d, sem_e, sem_f, *gsems = rest
    copies = shards // seqs
    index, head = lax.axis_index("seq"), lax.axis_index("head")
    lane = lax.rem(index, copies)
    row = lax.div(index, copies)
    active = lane == lax.rem(head, copies)
    slot = lax.div(head, copies)
    pick_barrier([("head", heads), ("seq", shards)])

    def first(t, to_do):
        there = lax.rem(head + t, heads)
        copy = remote(
            o_ref.at[there], blocks.at[slot], sem_a.at[t], sem_b.at[slot], {"head": there}
        )
        to_do(copy)

    keep = pltpu.make_async_copy(o_ref.at[head], blocks.at[slot], sem_b.at[slot])

    @pl.when(active)
    def _():
        keep.start()
        lax.fori_loop(1, heads, lambda t, c: (first(t, lambda copy: copy.start()), c)[1], 0)

    size = blocks.shape[2]
    count = blocks.shape[0]
    for i in range(count):
        pltpu.make_async_copy(o_ref.at[0], blocks.at[i], sem_b.at[i]).wait()
    place = lane * seqs + row
    joined[place] = jnp.concatenate([blocks[i] for i in range(count)], 1)

    sends = []
    for t in range(1, shards):
        there = lax.rem(index + t, shards)
        copy = remote(
            joined.at[place], joined.at[place], sem_c.at[t], sem_d.at[place], {"seq": there}
        )
        copy.start()
        sends.append(copy)
    for t in range(1, shards):
        source = lax.rem(index + shards - t, shards)
        came = lax.rem(source, copies) * seqs + lax.div(source, copies)
        pltpu.make_async_copy(joined.at[came], joined.at[came], sem_d.at[came]).wait()
    rows = joined.shape[1]
    inner = joined.shape[2]
    total = sum(
        jnp.dot(
            joined[pl.ds(i * seqs, seqs)].reshape(seqs * rows, inner),
            w_ref[i],
            preferred_element_type=F32,
        )
        for i in range(copies)
    )
    delta[...] = total.reshape(delta.shape)

    mine = pltpu.make_async_copy(delta.at[:, index], parts.at[index], sem_f.at[index])
    mine.start()
    for t in range(1, shards):
        there = lax.rem(index + t, shards)
        copy = remote(
            delta.at[:, there], parts.at[index], sem_e.at[t], sem_f.at[index], {"seq": there}
        )
        copy.start()
        sends.append(copy)
    for i in range(shards):
        pltpu.make_async_copy(delta.at[:, 0], parts.at[i], sem_f.at[i]).wait()
    cut = parts.shape[3]
    tokens = result.shape[0] * result.shape[1]
    for i in range(shards):
        columns = slice(i * cut, (i + 1) * cut)
        summed = local_ref[:, :, columns].astype(F32) + parts[i].reshape(
            result.shape[0], result.shape[1], cut
        )
        result[:, :, columns] = summed.astype(BF)
    if gathers:
        gather_blocks(result, full, *gsems)
    for copy in sends:
        copy.wait_send()

    @pl.when(active)
    def _():
        lax.fori_loop(1, heads, lambda t, c: (first(t, lambda copy: copy.wait_send()), c)[1], 0)


def run_out(o, sliced, local, seqs, gathers, number):
    heads, shards = lax.axis_size("head"), lax.axis_size("seq")
    copies = shards // seqs
    _, rows, size = o.shape
    cut = sliced.shape[2]
    count = heads // copies
    vmem = pl.BlockSpec(memory_space=pltpu.VMEM)
    shape = jax.ShapeDtypeStruct(local.shape, BF)
    out_shape, out_specs = [shape], [vmem]
    if gathers:
        out_shape.append(jax.ShapeDtypeStruct((heads, *local.shape), BF))
        out_specs.append(pl.BlockSpec(memory_space=pl.ANY))
    return pl.pallas_call(
        functools.partial(out_kernel, heads, shards, seqs, gathers),
        out_shape=out_shape,
        in_specs=[vmem] * 3,
        out_specs=out_specs,
        scratch_shapes=[
            pltpu.VMEM((count, rows, size), BF),
            pltpu.VMEM((shards, rows, count * size), BF),
            pltpu.VMEM((seqs, shards, rows // shards, cut), F32),
            pltpu.VMEM((shards, seqs, rows // shards, cut), F32),
            pltpu.SemaphoreType.DMA((heads,)),
            pltpu.SemaphoreType.DMA((count,)),
            pltpu.SemaphoreType.DMA((shards,)),
            pltpu.SemaphoreType.DMA((shards,)),
            pltpu.SemaphoreType.DMA((shards,)),
            pltpu.SemaphoreType.DMA((shards,)),
            *(gather_sems(heads) if gathers else []),
        ],
        compiler_params=pltpu.CompilerParams(
            vmem_limit_bytes=40 * 2**20, collective_id=number, has_side_effects=True
        ),
        name="out_gather" if gathers else "out_last",
    )(o, sliced, local)


def body(
    tokens,
    qkv_weight,
    rate_weight,
    first_init,
    first_bias,
    second_init,
    second_bias,
    norm_gain,
    norm_bias,
    out_weight,
):
    seqs, rows_here, width = tokens.shape
    shards = lax.axis_size("seq")
    heads = lax.axis_size("head")
    index = lax.axis_index("seq")
    cut = width // shards
    copies = shards // seqs

    def weights(layer):
        return jnp.concatenate(
            [
                qkv_weight[layer, 0],
                rate_weight[layer],
                jnp.zeros((HEAD_SIZE - 1, width), BF),
            ],
            0,
        )

    def params(layer):
        return (
            first_init[layer, 0],
            first_bias[layer],
            second_init[layer, 0],
            second_bias[layer].T,
            norm_gain[layer].T,
            norm_bias[layer].T,
        )

    def out_slice(layer):
        piece = lax.dynamic_slice_in_dim(out_weight[layer], index * cut, cut, 1)
        pieces = lax.all_gather(piece, "head", axis=0)
        size = piece.shape[0]
        pieces = pieces.reshape(heads // copies, copies, size, cut).transpose(1, 0, 2, 3)
        return pieces.reshape(copies, heads // copies * size, cut)

    def project(layer, full):
        flat = full.reshape(heads * seqs * rows_here, width)
        mixed = jnp.einsum("nd,ed->ne", flat, weights(layer), preferred_element_type=F32)
        return mixed.reshape(heads, seqs, rows_here, 4 * HEAD_SIZE)

    local = tokens.reshape(2, seqs * rows_here // 2, width)
    full = run_gather(local, 0)
    sliced = out_slice(0), out_slice(1)
    o = run_scan(True, 1, project(0, full), *params(0))
    middle, full = run_out(o, sliced[0], local, seqs, True, 2)
    o = run_scan(False, 3, project(1, full), *params(1))
    (result,) = run_out(o, sliced[1], middle, seqs, False, 4)
    return result.reshape(tokens.shape)


def solution(mesh):
    placed = (
        P(None, ("seq", "head"), None),
        P(None, "head", None, None),
        P(None, "head", None),
        P(None, "head", None, None),
        P(None, "head", None),
        P(None, "head", None, None),
        P(None, "head", None),
        P(None, "head", None),
        P(None, "head", None),
        P(None, "head", None),
    )
    return jax.shard_map(
        body, mesh=mesh, in_specs=placed, out_specs=P(None, ("seq", "head"), None), check_vma=False
    )
```

```python
import functools

import jax
import jax.numpy as jnp
from jax import lax
from jax.experimental import pallas as pl
from jax.experimental.pallas import tpu as pltpu
from jax.sharding import PartitionSpec as P

HEAD_SIZE = 64
MINI = 64
EPS = 1e-06
BF = jnp.bfloat16
F32 = jnp.float32


def dot(a, b, dims):
    return lax.dot_general(a, b, (dims, ((), ())), preferred_element_type=F32)


NN = ((1,), (0,))
NT = ((1,), (1,))
TN = ((0,), (0,))


def gelu_pair(z):
    coef = 0.7978845608028654
    zz = z * z
    cube = 0.044715 * coef * zz
    tanh_val = jnp.tanh(z * (coef + cube))
    half = 0.5 + 0.5 * tanh_val
    value = z * half
    slope = half + value * (1.0 - tanh_val) * (coef + 3.0 * cube)
    return value, slope


def split(x):
    high = x.astype(BF)
    return high, (x - high.astype(F32)).astype(BF)


def greet(peers):
    barrier = pltpu.get_barrier_semaphore()
    for where in peers:
        pl.semaphore_signal(
            barrier, inc=1, device_id=where, device_id_type=pl.DeviceIdType.MESH
        )
    pl.semaphore_wait(barrier, len(peers))


def others(axis, count):
    here = lax.axis_index(axis)
    return [{axis: lax.rem(here + t, count)} for t in range(1, count)]


class Place:
    def __init__(self, heads):
        self.ring = heads // 4
        self.head = lax.axis_index("head")
        self.x = lax.div(self.head, 2 * self.ring)
        self.z = lax.rem(lax.div(self.head, 2), self.ring)
        self.core = lax.rem(self.head, 2)
        self.up, self.down = self.name(self.x, self.z + 1), self.name(self.x, self.z - 1)
        self.beside = self.name(1 - self.x, self.z)
        self.twin = self.name(self.x, self.z, 1 - self.core)

    def name(self, x, z, core=None):
        core = self.core if core is None else core
        return (x * self.ring + lax.rem(z + 2 * self.ring, self.ring)) * 2 + core

    def near(self):
        return [{"head": to} for to in (self.up, self.down, self.beside, self.twin)]


def remote(src, dst, send_sem, recv_sem, where):
    return pltpu.make_async_remote_copy(
        src_ref=src,
        dst_ref=dst,
        send_sem=send_sem,
        recv_sem=recv_sem,
        device_id=where,
        device_id_type=pl.DeviceIdType.MESH,
    )


def scan_kernel(
    forward,
    layer,
    shards,
    heads,
    mixed_ref,
    weight_ref,
    w1_ref,
    b1_ref,
    w2_ref,
    b2_ref,
    g_ref,
    c_ref,
    o_ref,
    sliced_ref,
    chain,
    outs,
    send_sem,
    recv_sem,
    sliced_send,
    sliced_recv,
    w1d,
    b1,
    w2t,
    w2d,
    b2,
    g1h_p,
    g1l_p,
    g2h_p,
    g2l_p,
    th_p,
    tl_p,
    sh_p,
    sl_p,
):
    size, hidden = w1_ref.shape
    lanes = 2 * MINI
    half = MINI
    parts, seqs, per, _ = mixed_ref.shape
    copies = shards // seqs
    per = half // per
    minis = parts // per
    steps = shards * minis + 1
    index = lax.axis_index("seq")
    lane = lax.rem(lax.axis_index("head"), copies)
    row_here = lax.div(index, copies)
    active = lax.rem(index, copies) == lane

    at_head = Place(heads)
    greet(others("seq", shards) + at_head.near())
    twin = row_here * copies + 1 - lax.rem(index, copies)

    def piece(m, there, send, where):
        at = index * minis + m
        return (
            mixed_ref.at[pl.ds(m * per, per), there],
            chain.at[pl.ds(at * per, per)],
            send,
            recv_sem.at[at],
            where,
        )

    sends, crossing = [], []
    for m in range(minis) if forward else reversed(range(minis)):
        src, dst, sem, at, where = piece(m, row_here, send_sem.at[0, m], {"seq": twin})
        keep, across = pltpu.make_async_copy(src, dst, at), remote(src, dst, sem, at, where)
        pl.when(active)(keep.start)
        pl.when(jnp.logical_not(active))(across.start)
        crossing.append(across)
        for t in range(1, seqs):
            there = lax.rem(row_here + t, seqs)
            copy = remote(*piece(m, there, send_sem.at[t, m], {"seq": there * copies + lane}))
            copy.start()
            sends.append(copy)

    cut = sliced_ref.shape[3]
    columns = weight_ref.at[layer, :, pl.ds(pl.multiple_of(index * cut, cut), cut)]
    h = at_head
    me = h.x * h.ring + h.z
    keep = pltpu.make_async_copy(columns, sliced_ref.at[h.core, me], sliced_recv.at[h.core, me])
    keep.start()

    def pass_on(part, at, kind, to, src=None):
        spot = sliced_ref.at[part, at]
        return remote(
            spot if src is None else src,
            spot,
            sliced_send.at[kind, part, at],
            sliced_recv.at[part, at],
            {"head": to},
        )

    def landed(part, at):
        pltpu.make_async_copy(columns, sliced_ref.at[part, at], sliced_recv.at[part, at]).wait()

    to_twin = pass_on(h.core, me, 3, h.twin, columns)
    to_twin.start()

    def relay():
        begun = []

        def send(*what):
            copy = pass_on(*what)
            copy.start()
            begun.append(copy)

        spot = lambda x, z: x * h.ring + lax.rem(z + 2 * h.ring, h.ring)
        landed(h.core, me)
        landed(1 - h.core, me)
        for part, kind, to in (
            (1, 2, h.beside),
            (0, 0, h.up),
            (0, 1, h.down),
            (1, 0, h.up),
            (1, 1, h.down),
            (0, 2, h.beside),
        ):
            send(part, me, kind, to)
        last = h.ring // 2
        for k in range(last + 1):
            for sign, to, kind in ((1, h.up, 0), (-1, h.down, 1)):
                if (k == 0 or k == last) and sign < 0:
                    continue
                mine, other = spot(h.x, h.z - sign * k), spot(1 - h.x, h.z - sign * k)
                for part, at in ((0, mine), (1, mine), (1, other)):
                    if k == 0 and at is mine:
                        continue
                    landed(part, at)
                    if k == 0:
                        send(1, at, 0, h.up)
                        send(1, at, 1, h.down)
                    elif k < last - 1 or (k == last - 1 and sign > 0):
                        send(part, at, kind, to)
                    if part == 0:
                        send(0, at, 2, h.beside)
                    send(part, at, 3, h.twin)
            for off in (k, -k) if 0 < k < last else (k,):
                at = spot(1 - h.x, h.z + off)
                landed(0, at)
                send(0, at, 3, h.twin)
        for copy in begun:
            copy.wait_send()

    pl.when(jnp.logical_not(active))(relay)

    def place(j):
        j = jnp.clip(j, 0, steps - 2)
        return j if forward else steps - 2 - j

    def wait_for(at):
        pltpu.make_async_copy(
            mixed_ref.at[pl.ds(0, per), row_here], chain.at[pl.ds(at * per, per)], recv_sem.at[at]
        ).wait()

    w1d[...] = jnp.concatenate([w1_ref[...], w1_ref[...]], 0).T
    b1[...] = jnp.broadcast_to(b1_ref[...], (lanes, hidden)).T
    centred = w2_ref[...] - jnp.mean(w2_ref[...], axis=1, keepdims=True)
    w2d[...] = jnp.concatenate([centred, centred], 1)
    w2t[...] = centred.T
    b2[...] = jnp.broadcast_to(b2_ref[...] - jnp.mean(b2_ref[...]), (size, lanes))
    for ref in (g1h_p, g1l_p, g2h_p, g2l_p, th_p, tl_p, sh_p, sl_p):
        ref[...] = jnp.zeros_like(ref)

    row = lax.broadcasted_iota(jnp.int32, (lanes, lanes), 0) - half
    col = lax.broadcasted_iota(jnp.int32, (lanes, lanes), 1)
    seen = (row <= col) if forward else (row >= col)
    first_mask = (seen | (col >= half)).astype(F32)
    second_mask = (~seen & (col < half)).astype(F32)
    left = col[:size] < half
    low_half = lax.broadcasted_iota(jnp.int32, (hidden, lanes), 1) < half
    gain = jnp.broadcast_to(g_ref[...], (size, lanes))
    shift = jnp.broadcast_to(c_ref[...], (size, lanes))
    gain2 = gain * gain
    ones = jnp.ones((lanes, lanes), BF)
    zeros = jnp.zeros((lanes, lanes), BF)
    blank = jnp.zeros((half, lanes), BF)

    def stacked(doubled):
        high = doubled.astype(BF)
        low = (doubled - high.astype(F32)).astype(BF)
        return jnp.concatenate([jnp.where(low_half, high, low), high], 1)

    def step(j, carry):
        @pl.when(j < steps - 1)
        def _():
            wait_for(place(j))

        before, now = place(j - 1), place(j)
        old = chain[pl.ds(before * per, per)].reshape(half, 4 * size)
        new = chain[pl.ds(now * per, per)].reshape(half, 4 * size)
        turned = jnp.concatenate([old[:, :lanes], new[:, :lanes]], 0).T
        s = jnp.where(left, turned[:size], turned[size:])
        turned = jnp.concatenate([old[:, lanes:], new[:, lanes:]], 0).T
        target = turned[:size] - s
        rate = jnp.where(
            left[:1], 0.0, jax.nn.sigmoid(turned[size : size + 1]) * (1.0 / HEAD_SIZE)
        )
        sh, sl = split(s)
        shp, slp = sh_p[...], sl_p[...]
        g1h, g1l = g1h_p[...], g1l_p[...]
        g2h, g2l = g2h_p[...], g2l_p[...]
        thp, tlp = th_p[...], tl_p[...]
        g1s = jnp.concatenate([g1h, g1l, g1h], 1)
        g2s = jnp.concatenate([g2h, g2l, g2h], 1)
        w1_old, b1_old = w1d[...], b1[...]
        w2t_new = w2t[...] - dot(g2s, jnp.concatenate([thp, thp, tlp], 1), NT)
        g2dh = jnp.concatenate([g2h, g2h], 0)
        g2dl = jnp.concatenate([g2l, g2l], 0)
        w2d_new = w2d[...] - dot(
            jnp.concatenate([thp, tlp, thp], 1), jnp.concatenate([g2dh, g2dh, g2dl], 1), NT
        )
        b2_new = b2[...] - jnp.sum(g2h.astype(F32) + g2l.astype(F32), axis=1, keepdims=True)
        w2t[...] = w2t_new
        w2d[...] = w2d_new
        b2[...] = b2_new
        sd_high = jnp.concatenate([shp, shp, ones], 0)
        sd_low = jnp.concatenate([slp, slp, zeros], 0)
        change = dot(g1s, jnp.concatenate([sd_high, sd_high, sd_low], 1), NT)
        w1d[...] = w1_old - change[:, :lanes]
        b1[...] = b1_old - change[:, lanes:]
        pair = dot(
            jnp.concatenate([shp, slp, shp], 0), jnp.concatenate([sh, sh, sl], 0), TN
        )
        ph, pl_ = split((pair + 1.0) * first_mask)
        z = (
            dot(stacked(w1_old), jnp.concatenate([sh, sh, sl, blank], 0), NN)
            + b1_old
            - dot(g1s, jnp.concatenate([ph, ph, pl_], 0), NN)
        )
        value, slope = gelu_pair(z)
        th, tl = split(value)
        w2h, w2l = split(w2t_new)
        z2 = (
            dot(
                jnp.concatenate([w2h, w2l, w2h], 1), jnp.concatenate([th, th, tl], 0), NN
            )
            + b2_new
        )
        cross = dot(
            jnp.concatenate([thp, tlp, thp], 0), jnp.concatenate([th, th, tl], 0), TN
        )
        ch, cl = split((cross + 1.0) * second_mask)
        z2o = z2 + dot(g2s, jnp.concatenate([ch, ch, cl], 0), NN)
        d0 = gain * (shift - target)
        zz = z2 * z2
        s_zz = jnp.sum(zz, axis=0, keepdims=True)
        s_g = jnp.sum(gain2 * z2, axis=0, keepdims=True)
        s_gzz = jnp.sum(gain2 * zz, axis=0, keepdims=True)
        s_dz = jnp.sum(d0 * z2, axis=0, keepdims=True)
        s_d = jnp.sum(d0, axis=0, keepdims=True)
        inv = lax.rsqrt(s_zz * (1.0 / size) + EPS)
        sum_h = inv * s_g + s_d
        sum_hn = inv * (inv * s_gzz + s_dz)
        n = z2 * inv
        scale = inv * rate
        g2h_n, g2l_n = split(scale * (gain2 * n + d0 - (sum_h + n * sum_hn) * (1.0 / size)))
        g1 = (
            dot(stacked(w2d_new), jnp.concatenate([g2h_n, g2h_n, g2l_n, blank], 0), NN) * slope
        )
        g1h_n, g1l_n = split(g1)
        s_oo = jnp.sum(z2o * z2o, axis=0, keepdims=True)
        no = z2o * lax.rsqrt(s_oo * (1.0 / size) + EPS)
        done = (s + gain * no + shift).T[:half].reshape(per, half // per, size)
        outs[pl.ds(lax.rem(before, minis) * per, per), lax.div(before, minis)] = done
        g1h_p[...] = g1h_n
        g1l_p[...] = g1l_n
        g2h_p[...] = g2h_n
        g2l_p[...] = g2l_n
        th_p[...] = th
        tl_p[...] = tl
        sh_p[...] = sh
        sl_p[...] = sl
        return carry

    @pl.when(active)
    def _():
        lax.fori_loop(0, steps, step, 0)
        o_ref[...] = outs[...].reshape(o_ref.shape).astype(BF)

    @pl.when(jnp.logical_not(active))
    def _():
        for across in crossing:
            across.wait_send()

    for copy in sends:
        copy.wait_send()

    to_twin.wait_send()

    @pl.when(active)
    def _():
        def settle(at, carry):
            landed(0, at)
            landed(1, at)
            return carry

        lax.fori_loop(0, heads // 2, settle, 0)


def run_scan(forward, layer, number, mixed, out_weight, w1, b1, w2, b2, g, c):
    parts, seqs, rows, width = mixed.shape
    shards, heads = lax.axis_size("seq"), lax.axis_size("head")
    minis = parts * rows // MINI
    copies = shards // seqs
    cut = out_weight.shape[2] // shards
    size, hidden = w1.shape
    lanes = 2 * MINI
    vmem = pl.BlockSpec(memory_space=pltpu.VMEM)
    pair = lambda shape: [pltpu.VMEM(shape, BF)] * 2
    return pl.pallas_call(
        functools.partial(scan_kernel, forward, layer, shards, heads),
        out_shape=[
            jax.ShapeDtypeStruct((parts, shards * rows, size), BF),
            jax.ShapeDtypeStruct((copies, heads // copies, size, cut), BF),
        ],
        in_specs=[pl.BlockSpec(memory_space=pl.ANY)] * 2 + [vmem] * 6,
        out_specs=[vmem, pl.BlockSpec(memory_space=pl.ANY)],
        scratch_shapes=[
            pltpu.VMEM((shards * parts, rows, width), F32),
            pltpu.VMEM((parts, shards, rows, size), F32),
            pltpu.SemaphoreType.DMA((seqs, minis)),
            pltpu.SemaphoreType.DMA((shards * minis,)),
            pltpu.SemaphoreType.DMA((4, 2, heads // 2)),
            pltpu.SemaphoreType.DMA((2, heads // 2)),
            pltpu.VMEM((hidden, lanes), F32),
            pltpu.VMEM((hidden, lanes), F32),
            pltpu.VMEM((size, hidden), F32),
            pltpu.VMEM((hidden, lanes), F32),
            pltpu.VMEM((size, lanes), F32),
            *pair((hidden, lanes)),
            *pair((size, lanes)),
            *pair((hidden, lanes)),
            *pair((size, lanes)),
        ],
        compiler_params=pltpu.CompilerParams(
            vmem_limit_bytes=40 * 2**20, collective_id=number, has_side_effects=True
        ),
        cost_estimate=pl.CostEstimate(
            flops=33 * 2 * 3008 * 65536, bytes_accessed=2 * 2**20, transcendentals=0
        ),
        name="scan_fwd" if forward else "scan_rev",
    )(mixed, out_weight, w1, b1, w2, b2, g, c)


def gather_project(layer, local, qkv_ref, rate_ref, mixed, full, weight, own_sem, send_sem, recv_sem):
    ring = full.shape[0]
    h = Place(4 * ring)
    x, z, core, name = h.x, h.z, h.core, h.name
    up, down, beside, twin = h.up, h.down, h.beside, h.twin
    here, across = 2 * x + core, 2 * (1 - x) + core
    last = ring // 2
    started = []

    def spot(off):
        off = (off + last - 1) % ring - last + 1
        return 2 * off - 1 if off > 0 else -2 * off

    def send(at, which, part, kind, to, to_at=None, src=None):
        to_at = at if to_at is None else to_at
        copy = remote(
            full.at[at, which, part] if src is None else src,
            full.at[to_at, which, part],
            send_sem.at[kind, at, which, part],
            recv_sem.at[to_at, which, part],
            {"head": to},
        )
        copy.start()
        started.append(copy)

    def arrive(at, which, part):
        pltpu.make_async_copy(
            local.at[part], full.at[at, which, part], recv_sem.at[at, which, part]
        ).wait()

    own = pltpu.make_async_copy(local, full.at[0, here], own_sem.at[0])
    own.start()
    for kind, part, to, at in (
        (2, 1, beside, 0),
        (0, 0, up, spot(-1)),
        (1, 0, down, spot(1)),
        (0, 1, up, spot(-1)),
        (1, 1, down, spot(1)),
        (2, 0, beside, 0),
        (3, 0, twin, 0),
        (3, 1, twin, 0),
    ):
        send(0, here, part, kind, to, at, local.at[part])
    size = qkv_ref.shape[2]
    load = pltpu.make_async_copy(qkv_ref.at[layer, 0], weight.at[pl.ds(0, size)], own_sem.at[1])
    load.start()
    weight[size:] = jnp.broadcast_to(rate_ref[layer], (weight.shape[0] - size, weight.shape[1]))
    arrive(0, across, 1)
    send(0, across, 1, 0, up, spot(-1))
    send(0, across, 1, 1, down, spot(1))
    send(0, across, 1, 3, twin)
    arrive(0, across, 0)
    send(0, across, 0, 3, twin)
    load.wait()
    own.wait()

    def project(places, offsets):
        for at in places:
            for x_ in (0, 1):
                arrive(at, 2 * x_ + 1 - core, 0)
                arrive(at, 2 * x_ + 1 - core, 1)
        count = len(places)
        block = full[places[0] : places[0] + count]
        rows = block.shape[1] * block.shape[2] * block.shape[3]
        out = dot(block.reshape(count * rows, block.shape[4]), weight[...], NT)
        out = out.reshape(count, 2, 2, *mixed.shape[1:])
        for i, off in enumerate(offsets):
            for x_ in (0, 1):
                mixed[pl.ds(name(x_, z + off, 0), 2)] = out[i, x_]

    turn = 1 - 2 * core
    for k in range(1, last + 1):
        ways = ((1, up, 0), (-1, down, 1)) if k < last else ((1, None, 0),)
        for which, part in ((here, 0), (here, 1), (across, 1)):
            for sign, to, kind in ways:
                at = spot(-sign * k)
                arrive(at, which, part)
                if k < last - 1:
                    send(at, which, part, kind, to, spot(-sign * (k + 1)))
                if part == 0:
                    send(at, which, 0, 2, beside)
                send(at, which, part, 3, twin)
        if k == last - 1:
            to = name(x, z + turn, core)
            at = spot(k) + 1 - core
            for which, part in ((here, 0), (here, 1), (across, 1)):
                send(at, which, part, 0, to, spot(last))
        for off in (k, -k) if k < last else (k,):
            arrive(spot(off), across, 0)
            send(spot(off), across, 0, 3, twin)
        if k == 1:
            project((0,), (0,))
        else:
            project((2 * k - 3, 2 * k - 2), (k - 1, 1 - k))
    project((2 * last - 1,), (last,))
    for copy in started:
        copy.wait_send()


def gather_scratch(heads, width):
    return [
        pltpu.VMEM((heads // 4, 4, 2, 16, width), BF),
        pltpu.VMEM((4 * HEAD_SIZE, width), BF),
        pltpu.SemaphoreType.DMA((2,)),
        pltpu.SemaphoreType.DMA((4, heads // 4, 4, 2)),
        pltpu.SemaphoreType.DMA((heads // 4, 4, 2)),
    ]


def gather_kernel(heads, local, qkv_ref, rate_ref, mixed, *scratch):
    greet(Place(heads).near())
    gather_project(0, local, qkv_ref, rate_ref, mixed, *scratch)


def run_gather(local, qkv_weight, rate_weight, seqs, number):
    heads = lax.axis_size("head")
    parts, rows, width = local.shape
    anyspec = pl.BlockSpec(memory_space=pl.ANY)
    vmem = pl.BlockSpec(memory_space=pltpu.VMEM)
    return pl.pallas_call(
        functools.partial(gather_kernel, heads),
        out_shape=jax.ShapeDtypeStruct((heads, seqs, parts * rows // seqs, 4 * HEAD_SIZE), F32),
        in_specs=[vmem, anyspec, vmem],
        out_specs=vmem,
        scratch_shapes=gather_scratch(heads, width),
        compiler_params=pltpu.CompilerParams(
            vmem_limit_bytes=40 * 2**20, collective_id=number, has_side_effects=True
        ),
        name="gather_tokens",
    )(local, qkv_weight, rate_weight)


def out_kernel(
    heads,
    shards,
    seqs,
    gathers,
    o_ref,
    w_ref,
    local_ref,
    *rest,
):
    if gathers:
        qkv_ref, rate_ref, result, mixed, *rest = rest
    else:
        result, *rest = rest
    blocks, joined, delta, parts, sem_a, sem_b, sem_c, sem_d, sem_e, sem_f, *gsems = rest
    copies = shards // seqs
    index, head = lax.axis_index("seq"), lax.axis_index("head")
    lane = lax.rem(index, copies)
    row = lax.div(index, copies)
    active = lane == lax.rem(head, copies)
    slot = lax.div(head, copies)
    greet(others("head", heads) + others("seq", shards))

    def first(t, to_do):
        there = lax.rem(head + t, heads)
        copy = remote(
            o_ref.at[there], blocks.at[slot], sem_a.at[t], sem_b.at[slot], {"head": there}
        )
        to_do(copy)

    keep = pltpu.make_async_copy(o_ref.at[head], blocks.at[slot], sem_b.at[slot])

    @pl.when(active)
    def _():
        keep.start()
        lax.fori_loop(1, heads, lambda t, c: (first(t, lambda copy: copy.start()), c)[1], 0)

    size = blocks.shape[2]
    count = blocks.shape[0]
    for i in range(count):
        pltpu.make_async_copy(o_ref.at[0], blocks.at[i], sem_b.at[i]).wait()
    place = lane * seqs + row
    joined[place] = jnp.concatenate([blocks[i] for i in range(count)], 1)

    sends = []
    for t in range(1, shards):
        there = lax.rem(index + t, shards)
        copy = remote(
            joined.at[place], joined.at[place], sem_c.at[t], sem_d.at[place], {"seq": there}
        )
        copy.start()
        sends.append(copy)
    for t in range(1, shards):
        source = lax.rem(index + shards - t, shards)
        came = lax.rem(source, copies) * seqs + lax.div(source, copies)
        pltpu.make_async_copy(joined.at[came], joined.at[came], sem_d.at[came]).wait()
    rows = joined.shape[1]
    inner = joined.shape[2]
    total = sum(
        jnp.dot(
            joined[pl.ds(i * seqs, seqs)].reshape(seqs * rows, inner),
            w_ref[i].reshape(inner, w_ref.shape[3]),
            preferred_element_type=F32,
        )
        for i in range(copies)
    )
    delta[...] = total.reshape(delta.shape)

    mine = pltpu.make_async_copy(delta.at[:, index], parts.at[index], sem_f.at[index])
    mine.start()
    for t in range(1, shards):
        there = lax.rem(index + t, shards)
        copy = remote(
            delta.at[:, there], parts.at[index], sem_e.at[t], sem_f.at[index], {"seq": there}
        )
        copy.start()
        sends.append(copy)
    for i in range(shards):
        pltpu.make_async_copy(delta.at[:, 0], parts.at[i], sem_f.at[i]).wait()
    cut = parts.shape[3]
    tokens = result.shape[0] * result.shape[1]
    for i in range(shards):
        columns = slice(i * cut, (i + 1) * cut)
        summed = local_ref[:, :, columns].astype(F32) + parts[i].reshape(
            result.shape[0], result.shape[1], cut
        )
        result[:, :, columns] = summed.astype(BF)
    if gathers:
        gather_project(1, result, qkv_ref, rate_ref, mixed, *gsems)
    for copy in sends:
        copy.wait_send()

    @pl.when(active)
    def _():
        lax.fori_loop(1, heads, lambda t, c: (first(t, lambda copy: copy.wait_send()), c)[1], 0)


def run_out(o, sliced, local, seqs, number, *projections):
    heads, shards = lax.axis_size("head"), lax.axis_size("seq")
    copies = shards // seqs
    _, rows, size = o.shape
    cut = sliced.shape[3]
    gathers = len(projections) > 0
    count = heads // copies
    vmem = pl.BlockSpec(memory_space=pltpu.VMEM)
    shape = jax.ShapeDtypeStruct(local.shape, BF)
    out_shape, out_specs = [shape], [vmem]
    if gathers:
        out_shape.append(
            jax.ShapeDtypeStruct((heads, seqs, rows // shards, 4 * HEAD_SIZE), F32)
        )
        out_specs.append(vmem)
    return pl.pallas_call(
        functools.partial(out_kernel, heads, shards, seqs, gathers),
        out_shape=out_shape,
        in_specs=[vmem] * 3 + [pl.BlockSpec(memory_space=pl.ANY), vmem][: len(projections)],
        out_specs=out_specs,
        scratch_shapes=[
            pltpu.VMEM((count, rows, size), BF),
            pltpu.VMEM((shards, rows, count * size), BF),
            pltpu.VMEM((seqs, shards, rows // shards, cut), F32),
            pltpu.VMEM((shards, seqs, rows // shards, cut), F32),
            pltpu.SemaphoreType.DMA((heads,)),
            pltpu.SemaphoreType.DMA((count,)),
            pltpu.SemaphoreType.DMA((shards,)),
            pltpu.SemaphoreType.DMA((shards,)),
            pltpu.SemaphoreType.DMA((shards,)),
            pltpu.SemaphoreType.DMA((shards,)),
            *(gather_scratch(heads, local.shape[2]) if gathers else []),
        ],
        compiler_params=pltpu.CompilerParams(
            vmem_limit_bytes=40 * 2**20, collective_id=number, has_side_effects=True
        ),
        name="out_gather" if gathers else "out_last",
    )(o, sliced, local, *projections)


def body(
    tokens,
    qkv_weight,
    rate_weight,
    first_init,
    first_bias,
    second_init,
    second_bias,
    norm_gain,
    norm_bias,
    out_weight,
):
    seqs, rows_here, width = tokens.shape
    local = tokens.reshape(2, seqs * rows_here // 2, width)
    project = (qkv_weight, rate_weight)

    def params(layer):
        return (
            first_init[layer, 0],
            first_bias[layer],
            second_init[layer, 0],
            second_bias[layer].T,
            norm_gain[layer].T,
            norm_bias[layer].T,
        )

    mixed = run_gather(local, *project, seqs, 0)
    o, sliced = run_scan(True, 0, 1, mixed, out_weight, *params(0))
    middle, mixed = run_out(o, sliced, local, seqs, 2, *project)
    o, sliced = run_scan(False, 1, 3, mixed, out_weight, *params(1))
    (result,) = run_out(o, sliced, middle, seqs, 4)
    return result.reshape(tokens.shape)


def solution(mesh):
    placed = (
        P(None, ("seq", "head"), None),
        P(None, "head", None, None),
        P(None, "head", None),
        P(None, "head", None, None),
        P(None, "head", None),
        P(None, "head", None, None),
        P(None, "head", None),
        P(None, "head", None),
        P(None, "head", None),
        P(None, "head", None),
    )
    return jax.shard_map(
        body, mesh=mesh, in_specs=placed, out_specs=P(None, ("seq", "head"), None), check_vma=False
    )
```

```python
import functools

import jax
import jax.numpy as jnp
from jax import lax
from jax.experimental import pallas as pl
from jax.experimental.pallas import tpu as pltpu
from jax.sharding import PartitionSpec as P

HEAD_SIZE = 64
MINI = 64
EPS = 1e-06
BF = jnp.bfloat16
F32 = jnp.float32


def dot(a, b, dims):
    return lax.dot_general(a, b, (dims, ((), ())), preferred_element_type=F32)


NN = ((1,), (0,))
NT = ((1,), (1,))
TN = ((0,), (0,))


def gelu_pair(z):
    coef = 0.7978845608028654
    zz = z * z
    cube = 0.044715 * coef * zz
    tanh_val = jnp.tanh(z * (coef + cube))
    half = 0.5 + 0.5 * tanh_val
    value = z * half
    slope = half + value * (1.0 - tanh_val) * (coef + 3.0 * cube)
    return value, slope


def split(x):
    high = x.astype(BF)
    return high, (x - high.astype(F32)).astype(BF)


def greet(peers):
    barrier = pltpu.get_barrier_semaphore()
    for where in peers:
        pl.semaphore_signal(
            barrier, inc=1, device_id=where, device_id_type=pl.DeviceIdType.MESH
        )
    pl.semaphore_wait(barrier, len(peers))


def others(axis, count):
    here = lax.axis_index(axis)
    return [{axis: lax.rem(here + t, count)} for t in range(1, count)]


class Place:
    def __init__(self, heads):
        self.ring = heads // 4
        self.head = lax.axis_index("head")
        self.x = lax.div(self.head, 2 * self.ring)
        self.z = lax.rem(lax.div(self.head, 2), self.ring)
        self.core = lax.rem(self.head, 2)
        self.up, self.down = self.name(self.x, self.z + 1), self.name(self.x, self.z - 1)
        self.beside = self.name(1 - self.x, self.z)
        self.twin = self.name(self.x, self.z, 1 - self.core)

    def name(self, x, z, core=None):
        core = self.core if core is None else core
        return (x * self.ring + lax.rem(z + 2 * self.ring, self.ring)) * 2 + core

    def near(self):
        return [{"head": to} for to in (self.up, self.down, self.beside, self.twin)]


def remote(src, dst, send_sem, recv_sem, where):
    return pltpu.make_async_remote_copy(
        src_ref=src,
        dst_ref=dst,
        send_sem=send_sem,
        recv_sem=recv_sem,
        device_id=where,
        device_id_type=pl.DeviceIdType.MESH,
    )


def scan_phase(
    forward,
    layer,
    shards,
    heads,
    mixed_ref,
    weight_ref,
    w1_ref,
    b1_ref,
    w2_ref,
    b2_ref,
    g_ref,
    c_ref,
    o_ref,
    sliced_ref,
    chain,
    outs,
    send_sem,
    recv_sem,
    sliced_send,
    sliced_recv,
    w1d,
    b1,
    w2t,
    w2d,
    b2,
    g1h_p,
    g1l_p,
    g2h_p,
    g2l_p,
    th_p,
    tl_p,
    sh_p,
    sl_p,
):
    size, hidden = w1_ref.shape[2:]
    lanes = 2 * MINI
    half = MINI
    parts, seqs, per, _ = mixed_ref.shape
    copies = shards // seqs
    per = half // per
    minis = parts // per
    steps = shards * minis + 1
    index = lax.axis_index("seq")
    lane = lax.rem(lax.axis_index("head"), copies)
    row_here = lax.div(index, copies)
    active = lax.rem(index, copies) == lane

    at_head = Place(heads)
    twin = row_here * copies + 1 - lax.rem(index, copies)

    def piece(m, there, send, where):
        at = index * minis + m
        return (
            mixed_ref.at[pl.ds(m * per, per), there],
            chain.at[pl.ds(at * per, per)],
            send,
            recv_sem.at[at],
            where,
        )

    sends, keeps, crossing = [], [], []
    for m in range(minis) if forward else reversed(range(minis)):
        src, dst, sem, at, where = piece(m, row_here, send_sem.at[0, m], {"seq": twin})
        keeps.append(pltpu.make_async_copy(src, dst, at))
        crossing.append(remote(src, dst, sem, at, where))
        for t in range(1, seqs):
            there = lax.rem(row_here + t, seqs)
            sends.append(
                remote(*piece(m, there, send_sem.at[t, m], {"seq": there * copies + lane}))
            )

    turn = index if forward else shards - 1 - index
    release = jnp.maximum(2 * turn - 2, 0)

    def send_all():
        for m in range(minis):
            pl.when(jnp.logical_not(active))(crossing[m].start)
            for copy in sends[m * (seqs - 1) : (m + 1) * (seqs - 1)]:
                copy.start()

    @pl.when(active)
    def _():
        for copy in keeps:
            copy.start()

    pl.when(release == 0)(send_all)

    cut = sliced_ref.shape[3]
    columns = weight_ref.at[layer, :, pl.ds(pl.multiple_of(index * cut, cut), cut)]
    h = at_head
    me = h.x * h.ring + h.z
    keep = pltpu.make_async_copy(columns, sliced_ref.at[h.core, me], sliced_recv.at[h.core, me])
    keep.start()

    def pass_on(part, at, kind, to, src=None):
        spot = sliced_ref.at[part, at]
        return remote(
            spot if src is None else src,
            spot,
            sliced_send.at[kind, part, at],
            sliced_recv.at[part, at],
            {"head": to},
        )

    def landed(part, at):
        pltpu.make_async_copy(columns, sliced_ref.at[part, at], sliced_recv.at[part, at]).wait()

    to_twin = pass_on(h.core, me, 3, h.twin, columns)
    to_twin.start()

    def relay():
        begun = []

        def send(*what):
            copy = pass_on(*what)
            copy.start()
            begun.append(copy)

        spot = lambda x, z: x * h.ring + lax.rem(z + 2 * h.ring, h.ring)
        landed(h.core, me)
        landed(1 - h.core, me)
        for part, kind, to in (
            (1, 2, h.beside),
            (0, 0, h.up),
            (0, 1, h.down),
            (1, 0, h.up),
            (1, 1, h.down),
            (0, 2, h.beside),
        ):
            send(part, me, kind, to)
        last = h.ring // 2
        for k in range(last + 1):
            if k == 1:
                pl.when((release > 0) & (release <= 4))(send_all)
            if k == 2:
                pl.when(release > 4)(send_all)
            for sign, to, kind in ((1, h.up, 0), (-1, h.down, 1)):
                if (k == 0 or k == last) and sign < 0:
                    continue
                mine, other = spot(h.x, h.z - sign * k), spot(1 - h.x, h.z - sign * k)
                for part, at in ((0, mine), (1, mine), (1, other)):
                    if k == 0 and at is mine:
                        continue
                    landed(part, at)
                    if k == 0:
                        send(1, at, 0, h.up)
                        send(1, at, 1, h.down)
                    elif k < last - 1 or (k == last - 1 and sign > 0):
                        send(part, at, kind, to)
                    if part == 0:
                        send(0, at, 2, h.beside)
                    send(part, at, 3, h.twin)
            for off in (k, -k) if 0 < k < last else (k,):
                at = spot(1 - h.x, h.z + off)
                landed(0, at)
                send(0, at, 3, h.twin)
        for copy in begun:
            copy.wait_send()

    pl.when(jnp.logical_not(active))(relay)

    def place(j):
        j = jnp.clip(j, 0, steps - 2)
        return j if forward else steps - 2 - j

    def wait_for(at):
        pltpu.make_async_copy(
            mixed_ref.at[pl.ds(0, per), row_here], chain.at[pl.ds(at * per, per)], recv_sem.at[at]
        ).wait()

    column = lambda ref: jnp.broadcast_to(ref[layer], (lanes, ref.shape[2])).T
    w1d[...] = jnp.concatenate([w1_ref[layer, 0], w1_ref[layer, 0]], 0).T
    b1[...] = column(b1_ref)
    centred = w2_ref[layer, 0] - jnp.mean(w2_ref[layer, 0], axis=0, keepdims=True)
    w2d[...] = jnp.concatenate([centred, centred], 0).T
    w2t[...] = centred
    bias = column(b2_ref)
    b2[...] = bias - jnp.mean(bias, axis=0, keepdims=True)
    for ref in (g1h_p, g1l_p, g2h_p, g2l_p, th_p, tl_p, sh_p, sl_p):
        ref[...] = jnp.zeros_like(ref)

    row = lax.broadcasted_iota(jnp.int32, (lanes, lanes), 0) - half
    col = lax.broadcasted_iota(jnp.int32, (lanes, lanes), 1)
    seen = (row <= col) if forward else (row >= col)
    first_mask = (seen | (col >= half)).astype(F32)
    second_mask = (~seen & (col < half)).astype(F32)
    left = col[:size] < half
    low_half = lax.broadcasted_iota(jnp.int32, (hidden, lanes), 1) < half
    gain, shift = column(g_ref), column(c_ref)
    gain2 = gain * gain
    ones = jnp.ones((lanes, lanes), BF)
    zeros = jnp.zeros((lanes, lanes), BF)
    blank = jnp.zeros((half, lanes), BF)

    def stacked(doubled):
        high = doubled.astype(BF)
        low = (doubled - high.astype(F32)).astype(BF)
        return jnp.concatenate([jnp.where(low_half, high, low), high], 1)

    def step(j, carry):
        pl.when((j == release) & (j > 0))(send_all)

        @pl.when(j < steps - 1)
        def _():
            wait_for(place(j))

        before, now = place(j - 1), place(j)
        old = chain[pl.ds(before * per, per)].reshape(half, 4 * size)
        new = chain[pl.ds(now * per, per)].reshape(half, 4 * size)
        turned = jnp.concatenate([old[:, :lanes], new[:, :lanes]], 0).T
        s = jnp.where(left, turned[:size], turned[size:])
        turned = jnp.concatenate([old[:, lanes:], new[:, lanes:]], 0).T
        target = turned[:size] - s
        rate = jnp.where(
            left[:1], 0.0, jax.nn.sigmoid(turned[size : size + 1]) * (1.0 / HEAD_SIZE)
        )
        sh, sl = split(s)
        shp, slp = sh_p[...], sl_p[...]
        g1h, g1l = g1h_p[...], g1l_p[...]
        g2h, g2l = g2h_p[...], g2l_p[...]
        thp, tlp = th_p[...], tl_p[...]
        g1s = jnp.concatenate([g1h, g1l, g1h], 1)
        g2s = jnp.concatenate([g2h, g2l, g2h], 1)
        w1_old, b1_old = w1d[...], b1[...]
        w2t_new = w2t[...] - dot(g2s, jnp.concatenate([thp, thp, tlp], 1), NT)
        g2dh = jnp.concatenate([g2h, g2h], 0)
        g2dl = jnp.concatenate([g2l, g2l], 0)
        w2d_new = w2d[...] - dot(
            jnp.concatenate([thp, tlp, thp], 1), jnp.concatenate([g2dh, g2dh, g2dl], 1), NT
        )
        b2_new = b2[...] - jnp.sum(g2h.astype(F32) + g2l.astype(F32), axis=1, keepdims=True)
        w2t[...] = w2t_new
        w2d[...] = w2d_new
        b2[...] = b2_new
        sd_high = jnp.concatenate([shp, shp, ones], 0)
        sd_low = jnp.concatenate([slp, slp, zeros], 0)
        change = dot(g1s, jnp.concatenate([sd_high, sd_high, sd_low], 1), NT)
        w1d[...] = w1_old - change[:, :lanes]
        b1[...] = b1_old - change[:, lanes:]
        pair = dot(
            jnp.concatenate([shp, slp, shp], 0), jnp.concatenate([sh, sh, sl], 0), TN
        )
        ph, pl_ = split((pair + 1.0) * first_mask)
        z = (
            dot(stacked(w1_old), jnp.concatenate([sh, sh, sl, blank], 0), NN)
            + b1_old
            - dot(g1s, jnp.concatenate([ph, ph, pl_], 0), NN)
        )
        value, slope = gelu_pair(z)
        th, tl = split(value)
        w2h, w2l = split(w2t_new)
        z2 = (
            dot(
                jnp.concatenate([w2h, w2l, w2h], 1), jnp.concatenate([th, th, tl], 0), NN
            )
            + b2_new
        )
        cross = dot(
            jnp.concatenate([thp, tlp, thp], 0), jnp.concatenate([th, th, tl], 0), TN
        )
        ch, cl = split((cross + 1.0) * second_mask)
        z2o = z2 + dot(g2s, jnp.concatenate([ch, ch, cl], 0), NN)
        d0 = gain * (shift - target)
        zz = z2 * z2
        s_zz = jnp.sum(zz, axis=0, keepdims=True)
        s_g = jnp.sum(gain2 * z2, axis=0, keepdims=True)
        s_gzz = jnp.sum(gain2 * zz, axis=0, keepdims=True)
        s_dz = jnp.sum(d0 * z2, axis=0, keepdims=True)
        s_d = jnp.sum(d0, axis=0, keepdims=True)
        inv = lax.rsqrt(s_zz * (1.0 / size) + EPS)
        sum_h = inv * s_g + s_d
        sum_hn = inv * (inv * s_gzz + s_dz)
        n = z2 * inv
        scale = inv * rate
        g2h_n, g2l_n = split(scale * (gain2 * n + d0 - (sum_h + n * sum_hn) * (1.0 / size)))
        g1 = (
            dot(stacked(w2d_new), jnp.concatenate([g2h_n, g2h_n, g2l_n, blank], 0), NN) * slope
        )
        g1h_n, g1l_n = split(g1)
        s_oo = jnp.sum(z2o * z2o, axis=0, keepdims=True)
        no = z2o * lax.rsqrt(s_oo * (1.0 / size) + EPS)
        done = (s + gain * no + shift).T[:half].reshape(per, half // per, size)
        outs[pl.ds(lax.rem(before, minis) * per, per), lax.div(before, minis)] = done
        g1h_p[...] = g1h_n
        g1l_p[...] = g1l_n
        g2h_p[...] = g2h_n
        g2l_p[...] = g2l_n
        th_p[...] = th
        tl_p[...] = tl
        sh_p[...] = sh
        sl_p[...] = sl
        return carry

    @pl.when(active)
    def _():
        lax.fori_loop(0, steps, step, 0)
        o_ref[...] = outs[...].reshape(o_ref.shape).astype(BF)

    @pl.when(jnp.logical_not(active))
    def _():
        for across in crossing:
            across.wait_send()

    for copy in sends:
        copy.wait_send()

    to_twin.wait_send()

    @pl.when(active)
    def _():
        def settle(at, carry):
            landed(0, at)
            landed(1, at)
            return carry

        lax.fori_loop(0, heads // 2, settle, 0)


def gather_project(layer, local, qkv_ref, rate_ref, mixed, full, weight, own_sem, send_sem, recv_sem):
    ring = full.shape[0]
    h = Place(4 * ring)
    x, z, core, name = h.x, h.z, h.core, h.name
    up, down, beside, twin = h.up, h.down, h.beside, h.twin
    here, across = 2 * x + core, 2 * (1 - x) + core
    last = ring // 2
    started = []

    def spot(off):
        off = (off + last - 1) % ring - last + 1
        return 2 * off - 1 if off > 0 else -2 * off

    def send(at, which, part, kind, to, to_at=None, src=None):
        to_at = at if to_at is None else to_at
        copy = remote(
            full.at[at, which, part] if src is None else src,
            full.at[to_at, which, part],
            send_sem.at[kind, at, which, part],
            recv_sem.at[to_at, which, part],
            {"head": to},
        )
        copy.start()
        started.append(copy)

    def arrive(at, which, part):
        pltpu.make_async_copy(
            local.at[part], full.at[at, which, part], recv_sem.at[at, which, part]
        ).wait()

    own = pltpu.make_async_copy(local, full.at[0, here], own_sem.at[0])
    own.start()
    for kind, part, to, at in (
        (2, 1, beside, 0),
        (0, 0, up, spot(-1)),
        (1, 0, down, spot(1)),
        (0, 1, up, spot(-1)),
        (1, 1, down, spot(1)),
        (2, 0, beside, 0),
        (3, 0, twin, 0),
        (3, 1, twin, 0),
    ):
        send(0, here, part, kind, to, at, local.at[part])
    size = qkv_ref.shape[2]
    load = pltpu.make_async_copy(qkv_ref.at[layer, 0], weight.at[pl.ds(0, size)], own_sem.at[1])
    load.start()
    weight[size:] = jnp.broadcast_to(rate_ref[layer], (weight.shape[0] - size, weight.shape[1]))
    arrive(0, across, 1)
    send(0, across, 1, 0, up, spot(-1))
    send(0, across, 1, 1, down, spot(1))
    send(0, across, 1, 3, twin)
    arrive(0, across, 0)
    send(0, across, 0, 3, twin)
    load.wait()
    own.wait()

    def project(places, offsets):
        for at in places:
            for x_ in (0, 1):
                arrive(at, 2 * x_ + 1 - core, 0)
                arrive(at, 2 * x_ + 1 - core, 1)
        count = len(places)
        block = full[places[0] : places[0] + count]
        rows = block.shape[1] * block.shape[2] * block.shape[3]
        out = dot(block.reshape(count * rows, block.shape[4]), weight[...], NT)
        out = out.reshape(count, 2, 2, *mixed.shape[1:])
        for i, off in enumerate(offsets):
            for x_ in (0, 1):
                mixed[pl.ds(name(x_, z + off, 0), 2)] = out[i, x_]

    def hand_over(k):
        for off in (k, -k) if k < last else (k,):
            arrive(spot(off), across, 0)
            send(spot(off), across, 0, 3, twin)

    def project_at(k):
        if k == 1:
            project((0,), (0,))
        if k < last:
            project((2 * k - 1, 2 * k), (k, -k))
        else:
            project((2 * k - 1,), (k,))

    turn = 1 - 2 * core
    for k in range(1, last + 1):
        ways = ((1, up, 0), (-1, down, 1)) if k < last else ((1, None, 0),)
        for which, part in ((here, 0), (here, 1), (across, 1)):
            for sign, to, kind in ways:
                at = spot(-sign * k)
                arrive(at, which, part)
                if k < last - 1:
                    send(at, which, part, kind, to, spot(-sign * (k + 1)))
                if part == 0:
                    send(at, which, 0, 2, beside)
                send(at, which, part, 3, twin)
        if k == last - 1:
            to = name(x, z + turn, core)
            at = spot(k) + 1 - core
            for which, part in ((here, 0), (here, 1), (across, 1)):
                send(at, which, part, 0, to, spot(last))
        if k > 1:
            hand_over(k - 1)
        if k > 2:
            project_at(k - 2)
    hand_over(last)
    project_at(last - 1)
    project_at(last)
    for copy in started:
        copy.wait_send()


def out_phase(
    heads,
    shards,
    seqs,
    o_ref,
    w_ref,
    local_ref,
    result,
    blocks,
    joined,
    delta,
    parts,
    sem_a,
    sem_b,
    sem_c,
    sem_d,
    sem_e,
    sem_f,
):
    copies = shards // seqs
    index, head = lax.axis_index("seq"), lax.axis_index("head")
    lane = lax.rem(index, copies)
    row = lax.div(index, copies)
    active = lane == lax.rem(head, copies)
    slot = lax.div(head, copies)

    def first(t, to_do):
        there = lax.rem(head + t, heads)
        copy = remote(
            o_ref.at[there], blocks.at[slot], sem_a.at[t], sem_b.at[slot], {"head": there}
        )
        to_do(copy)

    keep = pltpu.make_async_copy(o_ref.at[head], blocks.at[slot], sem_b.at[slot])

    @pl.when(active)
    def _():
        keep.start()
        lax.fori_loop(1, heads, lambda t, c: (first(t, lambda copy: copy.start()), c)[1], 0)

    size = blocks.shape[2]
    count = blocks.shape[0]
    for i in range(count):
        pltpu.make_async_copy(o_ref.at[0], blocks.at[i], sem_b.at[i]).wait()
    place = lane * seqs + row
    joined[place] = jnp.concatenate([blocks[i] for i in range(count)], 1)

    sends = []
    for t in range(1, shards):
        there = lax.rem(index + t, shards)
        copy = remote(
            joined.at[place], joined.at[place], sem_c.at[t], sem_d.at[place], {"seq": there}
        )
        copy.start()
        sends.append(copy)
    for t in range(1, shards):
        source = lax.rem(index + shards - t, shards)
        came = lax.rem(source, copies) * seqs + lax.div(source, copies)
        pltpu.make_async_copy(joined.at[came], joined.at[came], sem_d.at[came]).wait()
    rows = joined.shape[1]
    inner = joined.shape[2]
    total = sum(
        jnp.dot(
            joined[pl.ds(i * seqs, seqs)].reshape(seqs * rows, inner),
            w_ref[i].reshape(inner, w_ref.shape[3]),
            preferred_element_type=F32,
        )
        for i in range(copies)
    )
    delta[...] = total.reshape(delta.shape)

    mine = pltpu.make_async_copy(delta.at[:, index], parts.at[index], sem_f.at[index])
    mine.start()
    for t in range(1, shards):
        there = lax.rem(index + t, shards)
        copy = remote(
            delta.at[:, there], parts.at[index], sem_e.at[t], sem_f.at[index], {"seq": there}
        )
        copy.start()
        sends.append(copy)
    for i in range(shards):
        pltpu.make_async_copy(delta.at[:, 0], parts.at[i], sem_f.at[i]).wait()
    cut = parts.shape[3]
    tokens = result.shape[0] * result.shape[1]
    for i in range(shards):
        columns = slice(i * cut, (i + 1) * cut)
        summed = local_ref[:, :, columns].astype(F32) + parts[i].reshape(
            result.shape[0], result.shape[1], cut
        )
        result[:, :, columns] = summed.astype(BF)
    for copy in sends:
        copy.wait_send()

    @pl.when(active)
    def _():
        lax.fori_loop(1, heads, lambda t, c: (first(t, lambda copy: copy.wait_send()), c)[1], 0)


def whole_kernel(heads, shards, seqs, counts, *refs):
    local, qkv_ref, rate_ref, weight_ref, *params = refs[:10]
    result = refs[10]
    rest = list(refs[11:])

    def take(count):
        taken = rest[:count]
        del rest[:count]
        return taken

    weight, outs, middle, load_sem = take(4)
    held = take(len(params))
    state = take(counts[0])
    loads = [
        pltpu.make_async_copy(src, dst, load_sem.at[i])
        for i, (src, dst) in enumerate(zip(params, held))
    ]
    for load in loads:
        load.start()
    greet(others("head", heads) + others("seq", shards))
    for layer in range(2):
        mixed, *gather = take(counts[1])
        sliced, o, *scan = take(counts[2])
        out = take(counts[3])
        source, target = (local, middle) if layer == 0 else (middle, result)
        full, *sems = gather
        gather_project(layer, source, qkv_ref, rate_ref, mixed, full, weight, *sems)
        chain, *scan_sems = scan
        if layer == 0:
            for load in loads:
                load.wait()
        scan_phase(
            layer == 0,
            layer,
            shards,
            heads,
            mixed,
            weight_ref,
            *held,
            o,
            sliced,
            chain,
            outs,
            *scan_sems,
            *state,
        )
        out_phase(heads, shards, seqs, o, sliced, source, target, *out)


def body(tokens, qkv_weight, rate_weight, *rest):
    *params, out_weight = rest
    seqs, rows, width = tokens.shape
    heads, shards = lax.axis_size("head"), lax.axis_size("seq")
    hidden = params[0].shape[3]
    size = HEAD_SIZE
    lanes = 2 * MINI
    copies = shards // seqs
    minis = heads * rows // MINI
    cut = width // shards
    count = heads // copies
    dma = pltpu.SemaphoreType.DMA
    pair = lambda shape: [pltpu.VMEM(shape, BF)] * 2
    local = tokens.reshape(2, seqs * rows // 2, width)
    params[2] = params[2].transpose(0, 1, 3, 2)
    state = [
        pltpu.VMEM((hidden, lanes), F32),
        pltpu.VMEM((hidden, lanes), F32),
        pltpu.VMEM((size, hidden), F32),
        pltpu.VMEM((hidden, lanes), F32),
        pltpu.VMEM((size, lanes), F32),
        *pair((hidden, lanes)),
        *pair((size, lanes)),
        *pair((hidden, lanes)),
        *pair((size, lanes)),
    ]
    gather = [
        pltpu.VMEM((heads, seqs, rows, 4 * size), F32),
        pltpu.VMEM((heads // 4, 4, *local.shape), BF),
        dma((2,)),
        dma((4, heads // 4, 4, 2)),
        dma((heads // 4, 4, 2)),
    ]
    scan = [
        pltpu.VMEM((copies, count, size, cut), BF),
        pltpu.VMEM((heads, shards * rows, size), BF),
        pltpu.VMEM((shards * heads, rows, 4 * size), F32),
        dma((seqs, minis)),
        dma((shards * minis,)),
        dma((4, 2, count)),
        dma((2, count)),
    ]
    out = [
        pltpu.VMEM((count, shards * rows, size), BF),
        pltpu.VMEM((shards, shards * rows, count * size), BF),
        pltpu.VMEM((seqs, shards, rows, cut), F32),
        pltpu.VMEM((shards, seqs, rows, cut), F32),
        dma((heads,)),
        dma((count,)),
        dma((shards,)),
        dma((shards,)),
        dma((shards,)),
        dma((shards,)),
    ]
    hbm = pl.BlockSpec(memory_space=pltpu.HBM)
    vmem = pl.BlockSpec(memory_space=pltpu.VMEM)
    counts = (len(state), len(gather), len(scan), len(out))
    result = pl.pallas_call(
        functools.partial(whole_kernel, heads, shards, seqs, counts),
        out_shape=jax.ShapeDtypeStruct(local.shape, BF),
        in_specs=[vmem, hbm, vmem, hbm] + [hbm] * 6,
        out_specs=vmem,
        scratch_shapes=[
            pltpu.VMEM((4 * size, width), BF),
            pltpu.VMEM((heads, shards, rows, size), F32),
            pltpu.VMEM(local.shape, BF),
            dma((len(params),)),
            *[pltpu.VMEM(param.shape, F32) for param in params],
            *state,
            *(gather + scan + out),
            *(gather + scan + out),
        ],
        compiler_params=pltpu.CompilerParams(
            vmem_limit_bytes=63 * 2**20, collective_id=0, has_side_effects=True
        ),
        name="two_layers",
    )(local, qkv_weight, rate_weight, out_weight, *params)
    return result.reshape(tokens.shape)


def solution(mesh):
    placed = (
        P(None, ("seq", "head"), None),
        P(None, "head", None, None),
        P(None, "head", None),
        P(None, "head", None, None),
        P(None, "head", None),
        P(None, "head", None, None),
        P(None, "head", None),
        P(None, "head", None),
        P(None, "head", None),
        P(None, "head", None),
    )
    return jax.shard_map(
        body, mesh=mesh, in_specs=placed, out_specs=P(None, ("seq", "head"), None), check_vma=False
    )
```

```python
import functools

import jax
import jax.numpy as jnp
from jax import lax
from jax.experimental import pallas as pl
from jax.experimental.pallas import tpu as pltpu
from jax.sharding import PartitionSpec as P

HEAD_SIZE = 64
MINI = 64
EPS = 1e-06
EARLY = 4
LAG = 7
BF = jnp.bfloat16
F32 = jnp.float32


def dot(a, b, dims):
    return lax.dot_general(a, b, (dims, ((), ())), preferred_element_type=F32)


NN = ((1,), (0,))
NT = ((1,), (1,))
TN = ((0,), (0,))


def gelu_pair(z):
    coef = 0.7978845608028654
    zz = z * z
    cube = 0.044715 * coef * zz
    tanh_val = jnp.tanh(z * (coef + cube))
    half = 0.5 + 0.5 * tanh_val
    value = z * half
    slope = half + value * (1.0 - tanh_val) * (coef + 3.0 * cube)
    return value, slope


def split(x):
    high = x.astype(BF)
    return high, (x - high.astype(F32)).astype(BF)


def greet(peers):
    barrier = pltpu.get_barrier_semaphore()
    for where in peers:
        pl.semaphore_signal(
            barrier, inc=1, device_id=where, device_id_type=pl.DeviceIdType.MESH
        )
    pl.semaphore_wait(barrier, len(peers))


def others(axis, count):
    here = lax.axis_index(axis)
    return [{axis: lax.rem(here + t, count)} for t in range(1, count)]


class Place:
    def __init__(self, heads):
        self.ring = heads // 4
        self.head = lax.axis_index("head")
        self.x = lax.div(self.head, 2 * self.ring)
        self.z = lax.rem(lax.div(self.head, 2), self.ring)
        self.core = lax.rem(self.head, 2)
        self.up, self.down = self.name(self.x, self.z + 1), self.name(self.x, self.z - 1)
        self.beside = self.name(1 - self.x, self.z)
        self.twin = self.name(self.x, self.z, 1 - self.core)

    def name(self, x, z, core=None):
        core = self.core if core is None else core
        return (x * self.ring + lax.rem(z + 2 * self.ring, self.ring)) * 2 + core

    def near(self):
        return [{"head": to} for to in (self.up, self.down, self.beside, self.twin)]


def remote(src, dst, send_sem, recv_sem, where):
    return pltpu.make_async_remote_copy(
        src_ref=src,
        dst_ref=dst,
        send_sem=send_sem,
        recv_sem=recv_sem,
        device_id=where,
        device_id_type=pl.DeviceIdType.MESH,
    )


def scan_phase(
    forward,
    layer,
    shards,
    heads,
    mixed_ref,
    weight_ref,
    w1_ref,
    b1_ref,
    w2_ref,
    b2_ref,
    g_ref,
    c_ref,
    early,
    early_start,
    early_step,
    sliced_ref,
    chain,
    outs,
    send_sem,
    recv_sem,
    sliced_send,
    sliced_recv,
    w1d,
    b1,
    w2t,
    w2d,
    b2,
    g1h_p,
    g1l_p,
    g2h_p,
    g2l_p,
    th_p,
    tl_p,
    sh_p,
    sl_p,
):
    size, hidden = w1_ref.shape[2:]
    lanes = 2 * MINI
    half = MINI
    parts, seqs, per, _ = mixed_ref.shape
    copies = shards // seqs
    per = half // per
    minis = parts // per
    steps = shards * minis + 1
    index = lax.axis_index("seq")
    lane = lax.rem(lax.axis_index("head"), copies)
    row_here = lax.div(index, copies)
    active = lax.rem(index, copies) == lane

    at_head = Place(heads)
    twin = row_here * copies + 1 - lax.rem(index, copies)

    def piece(m, there, send, where):
        at = index * minis + m
        return (
            mixed_ref.at[pl.ds(m * per, per), there],
            chain.at[pl.ds(at * per, per)],
            send,
            recv_sem.at[at],
            where,
        )

    sends, keeps, crossing = [], [], []
    for m in range(minis) if forward else reversed(range(minis)):
        src, dst, sem, at, where = piece(m, row_here, send_sem.at[0, m], {"seq": twin})
        keeps.append(pltpu.make_async_copy(src, dst, at))
        crossing.append(remote(src, dst, sem, at, where))
        for t in range(1, seqs):
            there = lax.rem(row_here + t, seqs)
            sends.append(
                remote(*piece(m, there, send_sem.at[t, m], {"seq": there * copies + lane}))
            )

    turn = index if forward else shards - 1 - index
    release = jnp.maximum(2 * turn - 2, 0)

    def send_all():
        for m in range(minis):
            pl.when(jnp.logical_not(active))(crossing[m].start)
            for copy in sends[m * (seqs - 1) : (m + 1) * (seqs - 1)]:
                copy.start()

    @pl.when(active)
    def _():
        for copy in keeps:
            copy.start()

    pl.when(release == 0)(send_all)

    cut = sliced_ref.shape[3]
    columns = weight_ref.at[layer, :, pl.ds(pl.multiple_of(index * cut, cut), cut)]
    h = at_head
    me = h.x * h.ring + h.z
    keep = pltpu.make_async_copy(columns, sliced_ref.at[h.core, me], sliced_recv.at[h.core, me])
    keep.start()

    def pass_on(part, at, kind, to, src=None):
        spot = sliced_ref.at[part, at]
        return remote(
            spot if src is None else src,
            spot,
            sliced_send.at[kind, part, at],
            sliced_recv.at[part, at],
            {"head": to},
        )

    def landed(part, at):
        pltpu.make_async_copy(columns, sliced_ref.at[part, at], sliced_recv.at[part, at]).wait()

    to_twin = pass_on(h.core, me, 3, h.twin, columns)
    to_twin.start()

    def relay():
        begun = []

        def send(*what):
            copy = pass_on(*what)
            copy.start()
            begun.append(copy)

        spot = lambda x, z: x * h.ring + lax.rem(z + 2 * h.ring, h.ring)
        landed(h.core, me)
        landed(1 - h.core, me)
        for part, kind, to in (
            (1, 2, h.beside),
            (0, 0, h.up),
            (0, 1, h.down),
            (1, 0, h.up),
            (1, 1, h.down),
            (0, 2, h.beside),
        ):
            send(part, me, kind, to)
        last = h.ring // 2
        for k in range(last + 1):
            if k == 1:
                pl.when((release > 0) & (release <= 4))(send_all)
            if k == 2:
                pl.when(release > 4)(send_all)
            for sign, to, kind in ((1, h.up, 0), (-1, h.down, 1)):
                if (k == 0 or k == last) and sign < 0:
                    continue
                mine, other = spot(h.x, h.z - sign * k), spot(1 - h.x, h.z - sign * k)
                for part, at in ((0, mine), (1, mine), (1, other)):
                    if k == 0 and at is mine:
                        continue
                    landed(part, at)
                    if k == 0:
                        send(1, at, 0, h.up)
                        send(1, at, 1, h.down)
                    elif k < last - 1 or (k == last - 1 and sign > 0):
                        send(part, at, kind, to)
                    if part == 0:
                        send(0, at, 2, h.beside)
                    send(part, at, 3, h.twin)
            for off in (k, -k) if 0 < k < last else (k,):
                at = spot(1 - h.x, h.z + off)
                landed(0, at)
                send(0, at, 3, h.twin)
        early.go_on()
        for copy in begun:
            copy.wait_send()

    pl.when(jnp.logical_not(active))(relay)

    def place(j):
        j = jnp.clip(j, 0, steps - 2)
        return j if forward else steps - 2 - j

    def wait_for(at):
        pltpu.make_async_copy(
            mixed_ref.at[pl.ds(0, per), row_here], chain.at[pl.ds(at * per, per)], recv_sem.at[at]
        ).wait()

    column = lambda ref: jnp.broadcast_to(ref[layer], (lanes, ref.shape[2])).T
    w1d[...] = jnp.concatenate([w1_ref[layer, 0], w1_ref[layer, 0]], 0).T
    b1[...] = column(b1_ref)
    centred = w2_ref[layer, 0] - jnp.mean(w2_ref[layer, 0], axis=0, keepdims=True)
    w2d[...] = jnp.concatenate([centred, centred], 0).T
    w2t[...] = centred
    bias = column(b2_ref)
    b2[...] = bias - jnp.mean(bias, axis=0, keepdims=True)
    for ref in (g1h_p, g1l_p, g2h_p, g2l_p, th_p, tl_p, sh_p, sl_p):
        ref[...] = jnp.zeros_like(ref)

    row = lax.broadcasted_iota(jnp.int32, (lanes, lanes), 0) - half
    col = lax.broadcasted_iota(jnp.int32, (lanes, lanes), 1)
    seen = (row <= col) if forward else (row >= col)
    first_mask = (seen | (col >= half)).astype(F32)
    second_mask = (~seen & (col < half)).astype(F32)
    left = col[:size] < half
    low_half = lax.broadcasted_iota(jnp.int32, (hidden, lanes), 1) < half
    gain, shift = column(g_ref), column(c_ref)
    gain2 = gain * gain
    ones = jnp.ones((lanes, lanes), BF)
    zeros = jnp.zeros((lanes, lanes), BF)
    blank = jnp.zeros((half, lanes), BF)

    def stacked(doubled):
        high = doubled.astype(BF)
        low = (doubled - high.astype(F32)).astype(BF)
        return jnp.concatenate([jnp.where(low_half, high, low), high], 1)

    def step(j, carry):
        pl.when((j == release) & (j > 0))(send_all)

        @pl.when(j == early_step)
        def _():
            early.begin(outs, early_start)

        pl.when(j == early_step + LAG)(early.go_on)

        @pl.when(j < steps - 1)
        def _():
            wait_for(place(j))

        before, now = place(j - 1), place(j)
        old = chain[pl.ds(before * per, per)].reshape(half, 4 * size)
        new = chain[pl.ds(now * per, per)].reshape(half, 4 * size)
        turned = jnp.concatenate([old[:, :lanes], new[:, :lanes]], 0).T
        s = jnp.where(left, turned[:size], turned[size:])
        turned = jnp.concatenate([old[:, lanes:], new[:, lanes:]], 0).T
        target = turned[:size] - s
        rate = jnp.where(
            left[:1], 0.0, jax.nn.sigmoid(turned[size : size + 1]) * (1.0 / HEAD_SIZE)
        )
        sh, sl = split(s)
        shp, slp = sh_p[...], sl_p[...]
        g1h, g1l = g1h_p[...], g1l_p[...]
        g2h, g2l = g2h_p[...], g2l_p[...]
        thp, tlp = th_p[...], tl_p[...]
        g1s = jnp.concatenate([g1h, g1l, g1h], 1)
        g2s = jnp.concatenate([g2h, g2l, g2h], 1)
        w1_old, b1_old = w1d[...], b1[...]
        w2t_new = w2t[...] - dot(g2s, jnp.concatenate([thp, thp, tlp], 1), NT)
        g2dh = jnp.concatenate([g2h, g2h], 0)
        g2dl = jnp.concatenate([g2l, g2l], 0)
        w2d_new = w2d[...] - dot(
            jnp.concatenate([thp, tlp, thp], 1), jnp.concatenate([g2dh, g2dh, g2dl], 1), NT
        )
        b2_new = b2[...] - jnp.sum(g2h.astype(F32) + g2l.astype(F32), axis=1, keepdims=True)
        w2t[...] = w2t_new
        w2d[...] = w2d_new
        b2[...] = b2_new
        sd_high = jnp.concatenate([shp, shp, ones], 0)
        sd_low = jnp.concatenate([slp, slp, zeros], 0)
        change = dot(g1s, jnp.concatenate([sd_high, sd_high, sd_low], 1), NT)
        w1d[...] = w1_old - change[:, :lanes]
        b1[...] = b1_old - change[:, lanes:]
        pair = dot(
            jnp.concatenate([shp, slp, shp], 0), jnp.concatenate([sh, sh, sl], 0), TN
        )
        ph, pl_ = split((pair + 1.0) * first_mask)
        z = (
            dot(stacked(w1_old), jnp.concatenate([sh, sh, sl, blank], 0), NN)
            + b1_old
            - dot(g1s, jnp.concatenate([ph, ph, pl_], 0), NN)
        )
        value, slope = gelu_pair(z)
        th, tl = split(value)
        w2h, w2l = split(w2t_new)
        z2 = (
            dot(
                jnp.concatenate([w2h, w2l, w2h], 1), jnp.concatenate([th, th, tl], 0), NN
            )
            + b2_new
        )
        cross = dot(
            jnp.concatenate([thp, tlp, thp], 0), jnp.concatenate([th, th, tl], 0), TN
        )
        ch, cl = split((cross + 1.0) * second_mask)
        z2o = z2 + dot(g2s, jnp.concatenate([ch, ch, cl], 0), NN)
        d0 = gain * (shift - target)
        zz = z2 * z2
        s_zz = jnp.sum(zz, axis=0, keepdims=True)
        s_g = jnp.sum(gain2 * z2, axis=0, keepdims=True)
        s_gzz = jnp.sum(gain2 * zz, axis=0, keepdims=True)
        s_dz = jnp.sum(d0 * z2, axis=0, keepdims=True)
        s_d = jnp.sum(d0, axis=0, keepdims=True)
        inv = lax.rsqrt(s_zz * (1.0 / size) + EPS)
        sum_h = inv * s_g + s_d
        sum_hn = inv * (inv * s_gzz + s_dz)
        n = z2 * inv
        scale = inv * rate
        g2h_n, g2l_n = split(scale * (gain2 * n + d0 - (sum_h + n * sum_hn) * (1.0 / size)))
        g1 = (
            dot(stacked(w2d_new), jnp.concatenate([g2h_n, g2h_n, g2l_n, blank], 0), NN) * slope
        )
        g1h_n, g1l_n = split(g1)
        s_oo = jnp.sum(z2o * z2o, axis=0, keepdims=True)
        no = z2o * lax.rsqrt(s_oo * (1.0 / size) + EPS)
        done = (s + gain * no + shift).T[:half].reshape(per, half // per, size)
        outs[pl.ds(lax.rem(before, minis) * per, per), lax.div(before, minis)] = done
        g1h_p[...] = g1h_n
        g1l_p[...] = g1l_n
        g2h_p[...] = g2h_n
        g2l_p[...] = g2l_n
        th_p[...] = th
        tl_p[...] = tl
        sh_p[...] = sh
        sl_p[...] = sl
        return carry

    @pl.when(active)
    def _():
        lax.fori_loop(0, steps, step, 0)

    @pl.when(jnp.logical_not(active))
    def _():
        for across in crossing:
            across.wait_send()

    for copy in sends:
        copy.wait_send()

    to_twin.wait_send()

    @pl.when(active)
    def _():
        def settle(at, carry):
            landed(0, at)
            landed(1, at)
            return carry

        lax.fori_loop(0, heads // 2, settle, 0)


def gather_project(layer, local, qkv_ref, rate_ref, mixed, full, weight, own_sem, send_sem, recv_sem):
    ring = full.shape[0]
    h = Place(4 * ring)
    x, z, core, name = h.x, h.z, h.core, h.name
    up, down, beside, twin = h.up, h.down, h.beside, h.twin
    here, across = 2 * x + core, 2 * (1 - x) + core
    last = ring // 2
    started = []

    def spot(off):
        off = (off + last - 1) % ring - last + 1
        return 2 * off - 1 if off > 0 else -2 * off

    def send(at, which, part, kind, to, to_at=None, src=None):
        to_at = at if to_at is None else to_at
        copy = remote(
            full.at[at, which, part] if src is None else src,
            full.at[to_at, which, part],
            send_sem.at[kind, at, which, part],
            recv_sem.at[to_at, which, part],
            {"head": to},
        )
        copy.start()
        started.append(copy)

    def arrive(at, which, part):
        pltpu.make_async_copy(
            local.at[part], full.at[at, which, part], recv_sem.at[at, which, part]
        ).wait()

    own = pltpu.make_async_copy(local, full.at[0, here], own_sem.at[0])
    own.start()
    for kind, part, to, at in (
        (2, 1, beside, 0),
        (0, 0, up, spot(-1)),
        (1, 0, down, spot(1)),
        (0, 1, up, spot(-1)),
        (1, 1, down, spot(1)),
        (2, 0, beside, 0),
        (3, 0, twin, 0),
        (3, 1, twin, 0),
    ):
        send(0, here, part, kind, to, at, local.at[part])
    size = qkv_ref.shape[2]
    load = pltpu.make_async_copy(qkv_ref.at[layer, 0], weight.at[pl.ds(0, size)], own_sem.at[1])
    load.start()
    weight[size:] = jnp.broadcast_to(rate_ref[layer], (weight.shape[0] - size, weight.shape[1]))
    arrive(0, across, 1)
    send(0, across, 1, 0, up, spot(-1))
    send(0, across, 1, 1, down, spot(1))
    send(0, across, 1, 3, twin)
    arrive(0, across, 0)
    send(0, across, 0, 3, twin)
    load.wait()
    own.wait()

    def project(places, offsets):
        for at in places:
            for x_ in (0, 1):
                arrive(at, 2 * x_ + 1 - core, 0)
                arrive(at, 2 * x_ + 1 - core, 1)
        count = len(places)
        block = full[places[0] : places[0] + count]
        rows = block.shape[1] * block.shape[2] * block.shape[3]
        out = dot(block.reshape(count * rows, block.shape[4]), weight[...], NT)
        out = out.reshape(count, 2, 2, *mixed.shape[1:])
        for i, off in enumerate(offsets):
            for x_ in (0, 1):
                mixed[pl.ds(name(x_, z + off, 0), 2)] = out[i, x_]

    def hand_over(k):
        for off in (k, -k) if k < last else (k,):
            arrive(spot(off), across, 0)
            send(spot(off), across, 0, 3, twin)

    def project_at(k):
        if k == 1:
            project((0,), (0,))
        if k < last:
            project((2 * k - 1, 2 * k), (k, -k))
        else:
            project((2 * k - 1,), (k,))

    turn = 1 - 2 * core
    for k in range(1, last + 1):
        ways = ((1, up, 0), (-1, down, 1)) if k < last else ((1, None, 0),)
        for which, part in ((here, 0), (here, 1), (across, 1)):
            for sign, to, kind in ways:
                at = spot(-sign * k)
                arrive(at, which, part)
                if k < last - 1:
                    send(at, which, part, kind, to, spot(-sign * (k + 1)))
                if part == 0:
                    send(at, which, 0, 2, beside)
                send(at, which, part, 3, twin)
        if k == last - 1:
            to = name(x, z + turn, core)
            at = spot(k) + 1 - core
            for which, part in ((here, 0), (here, 1), (across, 1)):
                send(at, which, part, 0, to, spot(last))
        if k > 1:
            hand_over(k - 1)
        if k > 2:
            project_at(k - 2)
    hand_over(last)
    project_at(last - 1)
    project_at(last)
    for copy in started:
        copy.wait_send()


class Exchange:
    def __init__(self, heads, shards, seqs, o, blocks, joined, sem_a, sem_b, sem_c, sem_d):
        self.heads, self.shards, self.seqs = heads, shards, seqs
        self.o, self.blocks, self.joined = o, blocks, joined
        self.sem_a, self.sem_b, self.sem_c, self.sem_d = sem_a, sem_b, sem_c, sem_d
        self.copies = shards // seqs
        self.index, self.head = lax.axis_index("seq"), lax.axis_index("head")
        self.slot = lax.div(self.head, self.copies)
        self.place = self.place_of(self.index)

    def place_of(self, index):
        return lax.rem(index, self.copies) * self.seqs + lax.div(index, self.copies)

    def first(self, t):
        there = lax.rem(self.head + t, self.heads)
        return remote(
            self.o.at[there],
            self.blocks.at[self.slot],
            self.sem_a.at[t],
            self.sem_b.at[self.slot],
            {"head": there},
        )

    def begin(self, outs, start):
        rows = self.o.shape[1] // outs.shape[2]
        self.o[...] = outs[:, start : start + rows].reshape(self.o.shape).astype(BF)
        pltpu.make_async_copy(
            self.o.at[self.head], self.blocks.at[self.slot], self.sem_b.at[self.slot]
        ).start()
        lax.fori_loop(1, self.heads, lambda t, c: (self.first(t).start(), c)[1], 0)

    def second(self, t):
        there = lax.rem(self.index + t, self.shards)
        spot = self.joined.at[self.place]
        return remote(spot, spot, self.sem_c.at[t], self.sem_d.at[self.place], {"seq": there})

    def go_on(self):
        count = self.blocks.shape[0]
        for i in range(count):
            pltpu.make_async_copy(self.o.at[0], self.blocks.at[i], self.sem_b.at[i]).wait()
        self.joined[self.place] = jnp.concatenate([self.blocks[i] for i in range(count)], 1)
        for t in range(1, self.shards):
            self.second(t).start()

    def finish(self):
        for t in range(1, self.shards):
            came = self.place_of(lax.rem(self.index + self.shards - t, self.shards))
            spot = self.joined.at[came]
            pltpu.make_async_copy(spot, spot, self.sem_d.at[came]).wait()

    def settle(self, active):
        for t in range(1, self.shards):
            self.second(t).wait_send()

        @pl.when(active)
        def _():
            lax.fori_loop(1, self.heads, lambda t, c: (self.first(t).wait_send(), c)[1], 0)


def out_phase(
    shards,
    seqs,
    portions,
    starts,
    outs,
    w_ref,
    local_ref,
    result,
    delta,
    parts,
    sem_e,
    sem_f,
):
    copies = shards // seqs
    index, head = lax.axis_index("seq"), lax.axis_index("head")
    active = lax.rem(index, copies) == lax.rem(head, copies)
    late = portions[1]

    @pl.when(active)
    def _():
        late.begin(outs, starts[1])

    def product(portion, start):
        portion.finish()
        joined = portion.joined
        rows, inner = joined.shape[1:]
        total = sum(
            jnp.dot(
                joined[pl.ds(i * seqs, seqs)].reshape(seqs * rows, inner),
                w_ref[i].reshape(inner, w_ref.shape[3]),
                preferred_element_type=F32,
            )
            for i in range(copies)
        )
        count = rows // delta.shape[2]
        delta[:, start : start + count] = total.reshape(seqs, count, *delta.shape[2:])

    product(portions[0], starts[0])
    late.go_on()
    product(late, starts[1])

    mine = pltpu.make_async_copy(delta.at[:, index], parts.at[index], sem_f.at[index])
    mine.start()
    sends = []
    for t in range(1, shards):
        there = lax.rem(index + t, shards)
        copy = remote(
            delta.at[:, there], parts.at[index], sem_e.at[t], sem_f.at[index], {"seq": there}
        )
        copy.start()
        sends.append(copy)
    for i in range(shards):
        pltpu.make_async_copy(delta.at[:, 0], parts.at[i], sem_f.at[i]).wait()
    cut = parts.shape[3]
    for i in range(shards):
        columns = slice(i * cut, (i + 1) * cut)
        summed = local_ref[:, :, columns].astype(F32) + parts[i].reshape(
            result.shape[0], result.shape[1], cut
        )
        result[:, :, columns] = summed.astype(BF)
    for copy in sends:
        copy.wait_send()
    for portion in portions:
        portion.settle(active)


def whole_kernel(heads, shards, seqs, counts, *refs):
    local, qkv_ref, rate_ref, weight_ref, *params = refs[:10]
    result = refs[10]
    rest = list(refs[11:])

    def take(count):
        taken = rest[:count]
        del rest[:count]
        return taken

    weight, outs, middle, load_sem = take(4)
    held = take(len(params))
    state = take(counts[0])
    loads = [
        pltpu.make_async_copy(src, dst, load_sem.at[i])
        for i, (src, dst) in enumerate(zip(params, held))
    ]
    for load in loads:
        load.start()
    greet(others("head", heads) + others("seq", shards))
    for layer in range(2):
        mixed, *gather = take(counts[1])
        sliced, *scan = take(counts[2])
        portions = [Exchange(heads, shards, seqs, *take(counts[3])) for _ in range(2)]
        out = take(counts[4])
        starts = (0, EARLY) if layer == 0 else (shards - EARLY, 0)
        source, target = (local, middle) if layer == 0 else (middle, result)
        full, *sems = gather
        gather_project(layer, source, qkv_ref, rate_ref, mixed, full, weight, *sems)
        chain, *scan_sems = scan
        if layer == 0:
            for load in loads:
                load.wait()
        scan_phase(
            layer == 0,
            layer,
            shards,
            heads,
            mixed,
            weight_ref,
            *held,
            portions[0],
            starts[0],
            EARLY * (heads * local.shape[0] * local.shape[1] // seqs // MINI) + 1,
            sliced,
            chain,
            outs,
            *scan_sems,
            *state,
        )
        out_phase(shards, seqs, portions, starts, outs, sliced, source, target, *out)


def body(tokens, qkv_weight, rate_weight, *rest):
    *params, out_weight = rest
    seqs, rows, width = tokens.shape
    heads, shards = lax.axis_size("head"), lax.axis_size("seq")
    hidden = params[0].shape[3]
    size = HEAD_SIZE
    lanes = 2 * MINI
    copies = shards // seqs
    minis = heads * rows // MINI
    cut = width // shards
    count = heads // copies
    dma = pltpu.SemaphoreType.DMA
    pair = lambda shape: [pltpu.VMEM(shape, BF)] * 2
    local = tokens.reshape(2, seqs * rows // 2, width)
    params[2] = params[2].transpose(0, 1, 3, 2)
    state = [
        pltpu.VMEM((hidden, lanes), F32),
        pltpu.VMEM((hidden, lanes), F32),
        pltpu.VMEM((size, hidden), F32),
        pltpu.VMEM((hidden, lanes), F32),
        pltpu.VMEM((size, lanes), F32),
        *pair((hidden, lanes)),
        *pair((size, lanes)),
        *pair((hidden, lanes)),
        *pair((size, lanes)),
    ]
    gather = [
        pltpu.VMEM((heads, seqs, rows, 4 * size), F32),
        pltpu.VMEM((heads // 4, 4, *local.shape), BF),
        dma((2,)),
        dma((4, heads // 4, 4, 2)),
        dma((heads // 4, 4, 2)),
    ]
    scan = [
        pltpu.VMEM((copies, count, size, cut), BF),
        pltpu.VMEM((shards * heads, rows, 4 * size), F32),
        dma((seqs, minis)),
        dma((shards * minis,)),
        dma((4, 2, count)),
        dma((2, count)),
    ]
    portion = lambda many: [
        pltpu.VMEM((heads, many * rows, size), BF),
        pltpu.VMEM((count, many * rows, size), BF),
        pltpu.VMEM((shards, many * rows, count * size), BF),
        dma((heads,)),
        dma((count,)),
        dma((shards,)),
        dma((shards,)),
    ]
    out = [
        pltpu.VMEM((seqs, shards, rows, cut), F32),
        pltpu.VMEM((shards, seqs, rows, cut), F32),
        dma((shards,)),
        dma((shards,)),
    ]
    layer = gather + scan + portion(EARLY) + portion(shards - EARLY) + out
    hbm = pl.BlockSpec(memory_space=pltpu.HBM)
    vmem = pl.BlockSpec(memory_space=pltpu.VMEM)
    counts = (len(state), len(gather), len(scan), len(portion(1)), len(out))
    result = pl.pallas_call(
        functools.partial(whole_kernel, heads, shards, seqs, counts),
        out_shape=jax.ShapeDtypeStruct(local.shape, BF),
        in_specs=[vmem, hbm, vmem, hbm] + [hbm] * 6,
        out_specs=vmem,
        scratch_shapes=[
            pltpu.VMEM((4 * size, width), BF),
            pltpu.VMEM((heads, shards, rows, size), F32),
            pltpu.VMEM(local.shape, BF),
            dma((len(params),)),
            *[pltpu.VMEM(param.shape, F32) for param in params],
            *state,
            *layer,
            *layer,
        ],
        compiler_params=pltpu.CompilerParams(
            vmem_limit_bytes=63 * 2**20, collective_id=0, has_side_effects=True
        ),
        name="two_layers",
    )(local, qkv_weight, rate_weight, out_weight, *params)
    return result.reshape(tokens.shape)


def solution(mesh):
    placed = (
        P(None, ("seq", "head"), None),
        P(None, "head", None, None),
        P(None, "head", None),
        P(None, "head", None, None),
        P(None, "head", None),
        P(None, "head", None, None),
        P(None, "head", None),
        P(None, "head", None),
        P(None, "head", None),
        P(None, "head", None),
    )
    return jax.shard_map(
        body, mesh=mesh, in_specs=placed, out_specs=P(None, ("seq", "head"), None), check_vma=False
    )
```

```python
import functools

import jax
import jax.numpy as jnp
from jax import lax
from jax.experimental import pallas as pl
from jax.experimental.pallas import tpu as pltpu
from jax.sharding import PartitionSpec as P

HEAD_SIZE = 64
MINI = 64
EPS = 1e-06
EARLY = 4
LAG = 7
BF = jnp.bfloat16
F32 = jnp.float32


def dot(a, b, dims):
    return lax.dot_general(a, b, (dims, ((), ())), preferred_element_type=F32)


NN = ((1,), (0,))
NT = ((1,), (1,))
TN = ((0,), (0,))


def gelu_pair(z):
    coef = 0.7978845608028654
    zz = z * z
    cube = 0.044715 * coef * zz
    tanh_val = jnp.tanh(z * (coef + cube))
    half = 0.5 + 0.5 * tanh_val
    value = z * half
    slope = half + value * (1.0 - tanh_val) * (coef + 3.0 * cube)
    return value, slope


def split(x):
    high = x.astype(BF)
    return high, (x - high.astype(F32)).astype(BF)


def greet(peers):
    barrier = pltpu.get_barrier_semaphore()
    for where in peers:
        pl.semaphore_signal(
            barrier, inc=1, device_id=where, device_id_type=pl.DeviceIdType.MESH
        )
    pl.semaphore_wait(barrier, len(peers))


def others(axis, count):
    here = lax.axis_index(axis)
    return [{axis: lax.rem(here + t, count)} for t in range(1, count)]


class Place:
    def __init__(self, heads):
        self.ring = heads // 4
        self.head = lax.axis_index("head")
        self.x = lax.div(self.head, 2 * self.ring)
        self.z = lax.rem(lax.div(self.head, 2), self.ring)
        self.core = lax.rem(self.head, 2)
        self.up, self.down = self.name(self.x, self.z + 1), self.name(self.x, self.z - 1)
        self.beside = self.name(1 - self.x, self.z)
        self.twin = self.name(self.x, self.z, 1 - self.core)

    def name(self, x, z, core=None):
        core = self.core if core is None else core
        return (x * self.ring + lax.rem(z + 2 * self.ring, self.ring)) * 2 + core

    def near(self):
        return [{"head": to} for to in (self.up, self.down, self.beside, self.twin)]


def remote(src, dst, send_sem, recv_sem, where):
    return pltpu.make_async_remote_copy(
        src_ref=src,
        dst_ref=dst,
        send_sem=send_sem,
        recv_sem=recv_sem,
        device_id=where,
        device_id_type=pl.DeviceIdType.MESH,
    )


def scan_phase(
    forward,
    layer,
    shards,
    heads,
    mixed_ref,
    weight_ref,
    w1_ref,
    b1_ref,
    w2_ref,
    b2_ref,
    g_ref,
    c_ref,
    early,
    early_start,
    early_step,
    sliced_ref,
    chain,
    outs,
    send_sem,
    recv_sem,
    sliced_send,
    sliced_recv,
    w1d,
    b1,
    w2t,
    w2d,
    b2,
    g1h_p,
    g1l_p,
    g2h_p,
    g2l_p,
    th_p,
    tl_p,
    sh_p,
    sl_p,
):
    size, hidden = w1_ref.shape[2:]
    lanes = 2 * MINI
    half = MINI
    parts, seqs, per, _ = mixed_ref.shape
    copies = shards // seqs
    per = half // per
    minis = parts // per
    steps = shards * minis + 1
    index = lax.axis_index("seq")
    lane = lax.rem(lax.axis_index("head"), copies)
    row_here = lax.div(index, copies)
    active = lax.rem(index, copies) == lane

    at_head = Place(heads)
    twin = row_here * copies + 1 - lax.rem(index, copies)

    def piece(m, there, send, where):
        at = index * minis + m
        return (
            mixed_ref.at[pl.ds(m * per, per), there],
            chain.at[pl.ds(at * per, per)],
            send,
            recv_sem.at[at],
            where,
        )

    sends, keeps, crossing = [], [], []
    for m in range(minis) if forward else reversed(range(minis)):
        src, dst, sem, at, where = piece(m, row_here, send_sem.at[0, m], {"seq": twin})
        keeps.append(pltpu.make_async_copy(src, dst, at))
        crossing.append(remote(src, dst, sem, at, where))
        for t in range(1, seqs):
            there = lax.rem(row_here + t, seqs)
            sends.append(
                remote(*piece(m, there, send_sem.at[t, m], {"seq": there * copies + lane}))
            )

    turn = index if forward else shards - 1 - index
    release = jnp.maximum(2 * turn - 2, 0)

    def send_all():
        for m in range(minis):
            pl.when(jnp.logical_not(active))(crossing[m].start)
            for copy in sends[m * (seqs - 1) : (m + 1) * (seqs - 1)]:
                copy.start()

    @pl.when(active)
    def _():
        for copy in keeps:
            copy.start()

    pl.when(release == 0)(send_all)

    cut = sliced_ref.shape[3]
    columns = weight_ref.at[layer, :, pl.ds(pl.multiple_of(index * cut, cut), cut)]
    h = at_head
    me = h.x * h.ring + h.z
    keep = pltpu.make_async_copy(columns, sliced_ref.at[h.core, me], sliced_recv.at[h.core, me])
    keep.start()

    def pass_on(part, at, kind, to, src=None):
        spot = sliced_ref.at[part, at]
        return remote(
            spot if src is None else src,
            spot,
            sliced_send.at[kind, part, at],
            sliced_recv.at[part, at],
            {"head": to},
        )

    def landed(part, at):
        pltpu.make_async_copy(columns, sliced_ref.at[part, at], sliced_recv.at[part, at]).wait()

    to_twin = pass_on(h.core, me, 3, h.twin, columns)
    to_twin.start()

    def relay():
        begun = []

        def send(*what):
            copy = pass_on(*what)
            copy.start()
            begun.append(copy)

        spot = lambda x, z: x * h.ring + lax.rem(z + 2 * h.ring, h.ring)
        landed(h.core, me)
        landed(1 - h.core, me)
        for part, kind, to in (
            (1, 2, h.beside),
            (0, 0, h.up),
            (0, 1, h.down),
            (1, 0, h.up),
            (1, 1, h.down),
            (0, 2, h.beside),
        ):
            send(part, me, kind, to)
        last = h.ring // 2
        for k in range(last + 1):
            if k == 1:
                pl.when((release > 0) & (release <= 4))(send_all)
            if k == 2:
                pl.when(release > 4)(send_all)
            for sign, to, kind in ((1, h.up, 0), (-1, h.down, 1)):
                if (k == 0 or k == last) and sign < 0:
                    continue
                mine, other = spot(h.x, h.z - sign * k), spot(1 - h.x, h.z - sign * k)
                for part, at in ((0, mine), (1, mine), (1, other)):
                    if k == 0 and at is mine:
                        continue
                    landed(part, at)
                    if k == 0:
                        send(1, at, 0, h.up)
                        send(1, at, 1, h.down)
                    elif k < last - 1 or (k == last - 1 and sign > 0):
                        send(part, at, kind, to)
                    if part == 0:
                        send(0, at, 2, h.beside)
                    send(part, at, 3, h.twin)
            for off in (k, -k) if 0 < k < last else (k,):
                at = spot(1 - h.x, h.z + off)
                landed(0, at)
                send(0, at, 3, h.twin)
        early.go_on()
        for copy in begun:
            copy.wait_send()

    pl.when(jnp.logical_not(active))(relay)

    def place(j):
        j = jnp.clip(j, 0, steps - 2)
        return j if forward else steps - 2 - j

    def wait_for(at):
        pltpu.make_async_copy(
            mixed_ref.at[pl.ds(0, per), row_here], chain.at[pl.ds(at * per, per)], recv_sem.at[at]
        ).wait()

    column = lambda ref: jnp.broadcast_to(ref[layer], (lanes, ref.shape[2])).T
    w1d[...] = jnp.concatenate([w1_ref[layer, 0], w1_ref[layer, 0]], 0).T
    b1[...] = column(b1_ref)
    centred = w2_ref[layer, 0] - jnp.mean(w2_ref[layer, 0], axis=0, keepdims=True)
    w2d[...] = jnp.concatenate([centred, centred], 0).T
    w2t[...] = centred
    bias = column(b2_ref)
    b2[...] = bias - jnp.mean(bias, axis=0, keepdims=True)
    for ref in (g1h_p, g1l_p, g2h_p, g2l_p, th_p, tl_p, sh_p, sl_p):
        ref[...] = jnp.zeros_like(ref)

    row = lax.broadcasted_iota(jnp.int32, (lanes, lanes), 0) - half
    col = lax.broadcasted_iota(jnp.int32, (lanes, lanes), 1)
    seen = (row <= col) if forward else (row >= col)
    first_mask = (seen | (col >= half)).astype(F32)
    second_mask = (~seen & (col < half)).astype(F32)
    left = col[:size] < half
    low_half = lax.broadcasted_iota(jnp.int32, (hidden, lanes), 1) < half
    gain, shift = column(g_ref), column(c_ref)
    gain2 = gain * gain
    ones = jnp.ones((lanes, lanes), BF)
    zeros = jnp.zeros((lanes, lanes), BF)
    blank = jnp.zeros((half, lanes), BF)

    def stacked(doubled):
        high = doubled.astype(BF)
        low = (doubled - high.astype(F32)).astype(BF)
        return jnp.concatenate([jnp.where(low_half, high, low), high], 1)

    def step(j, carry):
        pl.when((j == release) & (j > 0))(send_all)

        @pl.when(j == early_step)
        def _():
            early.begin(outs, early_start)

        pl.when(j == early_step + LAG)(early.go_on)

        @pl.when(j < steps - 1)
        def _():
            wait_for(place(j))

        before, now = place(j - 1), place(j)
        old = chain[pl.ds(before * per, per)].reshape(half, 4 * size)
        new = chain[pl.ds(now * per, per)].reshape(half, 4 * size)
        turned = jnp.concatenate([old[:, :lanes], new[:, :lanes]], 0).T
        s = jnp.where(left, turned[:size], turned[size:])
        turned = jnp.concatenate([old[:, lanes:], new[:, lanes:]], 0).T
        target = turned[:size] - s
        rate = jnp.where(
            left[:1], 0.0, jax.nn.sigmoid(turned[size : size + 1]) * (1.0 / HEAD_SIZE)
        )
        sh, sl = split(s)
        shp, slp = sh_p[...], sl_p[...]
        g1h, g1l = g1h_p[...], g1l_p[...]
        g2h, g2l = g2h_p[...], g2l_p[...]
        thp, tlp = th_p[...], tl_p[...]
        g1s = jnp.concatenate([g1h, g1l, g1h], 1)
        g2s = jnp.concatenate([g2h, g2l, g2h], 1)
        w1_old, b1_old = w1d[...], b1[...]
        w2t_new = w2t[...] - dot(g2s, jnp.concatenate([thp, thp, tlp], 1), NT)
        g2dh = jnp.concatenate([g2h, g2h], 0)
        g2dl = jnp.concatenate([g2l, g2l], 0)
        w2d_new = w2d[...] - dot(
            jnp.concatenate([thp, tlp, thp], 1), jnp.concatenate([g2dh, g2dh, g2dl], 1), NT
        )
        b2_new = b2[...] - jnp.sum(g2h.astype(F32) + g2l.astype(F32), axis=1, keepdims=True)
        w2t[...] = w2t_new
        w2d[...] = w2d_new
        b2[...] = b2_new
        sd_high = jnp.concatenate([shp, shp, ones], 0)
        sd_low = jnp.concatenate([slp, slp, zeros], 0)
        change = dot(g1s, jnp.concatenate([sd_high, sd_high, sd_low], 1), NT)
        w1d[...] = w1_old - change[:, :lanes]
        b1[...] = b1_old - change[:, lanes:]
        pair = dot(
            jnp.concatenate([shp, slp, shp], 0), jnp.concatenate([sh, sh, sl], 0), TN
        )
        ph, pl_ = split((pair + 1.0) * first_mask)
        z = (
            dot(stacked(w1_old), jnp.concatenate([sh, sh, sl, blank], 0), NN)
            + b1_old
            - dot(g1s, jnp.concatenate([ph, ph, pl_], 0), NN)
        )
        value, slope = gelu_pair(z)
        th, tl = split(value)
        w2h, w2l = split(w2t_new)
        z2 = (
            dot(
                jnp.concatenate([w2h, w2l, w2h], 1), jnp.concatenate([th, th, tl], 0), NN
            )
            + b2_new
        )
        cross = dot(
            jnp.concatenate([thp, tlp, thp], 0), jnp.concatenate([th, th, tl], 0), TN
        )
        ch, cl = split((cross + 1.0) * second_mask)
        z2o = z2 + dot(g2s, jnp.concatenate([ch, ch, cl], 0), NN)
        d0 = gain * (shift - target)
        zz = z2 * z2
        s_zz = jnp.sum(zz, axis=0, keepdims=True)
        s_g = jnp.sum(gain2 * z2, axis=0, keepdims=True)
        s_gzz = jnp.sum(gain2 * zz, axis=0, keepdims=True)
        s_dz = jnp.sum(d0 * z2, axis=0, keepdims=True)
        s_d = jnp.sum(d0, axis=0, keepdims=True)
        inv = lax.rsqrt(s_zz * (1.0 / size) + EPS)
        sum_h = inv * s_g + s_d
        sum_hn = inv * (inv * s_gzz + s_dz)
        n = z2 * inv
        scale = inv * rate
        g2h_n, g2l_n = split(scale * (gain2 * n + d0 - (sum_h + n * sum_hn) * (1.0 / size)))
        g1 = (
            dot(stacked(w2d_new), jnp.concatenate([g2h_n, g2h_n, g2l_n, blank], 0), NN) * slope
        )
        g1h_n, g1l_n = split(g1)
        s_oo = jnp.sum(z2o * z2o, axis=0, keepdims=True)
        no = z2o * lax.rsqrt(s_oo * (1.0 / size) + EPS)
        done = (s + gain * no + shift).T[:half].reshape(per, half // per, size)
        outs[pl.ds(lax.rem(before, minis) * per, per), lax.div(before, minis)] = done
        g1h_p[...] = g1h_n
        g1l_p[...] = g1l_n
        g2h_p[...] = g2h_n
        g2l_p[...] = g2l_n
        th_p[...] = th
        tl_p[...] = tl
        sh_p[...] = sh
        sl_p[...] = sl
        return carry

    @pl.when(active)
    def _():
        lax.fori_loop(0, steps, step, 0)

    @pl.when(jnp.logical_not(active))
    def _():
        for across in crossing:
            across.wait_send()

    for copy in sends:
        copy.wait_send()

    to_twin.wait_send()

    @pl.when(active)
    def _():
        def settle(at, carry):
            landed(0, at)
            landed(1, at)
            return carry

        lax.fori_loop(0, heads // 2, settle, 0)


def gather_project(layer, local, qkv_ref, rate_ref, mixed, full, weight, own_sem, send_sem, recv_sem):
    ring = full.shape[0]
    h = Place(4 * ring)
    x, z, core, name = h.x, h.z, h.core, h.name
    up, down, beside, twin = h.up, h.down, h.beside, h.twin
    here, across = 2 * x + core, 2 * (1 - x) + core
    last = ring // 2
    started = []

    def spot(off):
        off = (off + last - 1) % ring - last + 1
        return 2 * off - 1 if off > 0 else -2 * off

    def send(at, which, part, kind, to, to_at=None, src=None):
        to_at = at if to_at is None else to_at
        copy = remote(
            full.at[at, which, part] if src is None else src,
            full.at[to_at, which, part],
            send_sem.at[kind, at, which, part],
            recv_sem.at[to_at, which, part],
            {"head": to},
        )
        copy.start()
        started.append(copy)

    def arrive(at, which, part):
        pltpu.make_async_copy(
            local.at[part], full.at[at, which, part], recv_sem.at[at, which, part]
        ).wait()

    own = pltpu.make_async_copy(local, full.at[0, here], own_sem.at[0])
    own.start()
    for kind, part, to, at in (
        (2, 1, beside, 0),
        (0, 0, up, spot(-1)),
        (1, 0, down, spot(1)),
        (0, 1, up, spot(-1)),
        (1, 1, down, spot(1)),
        (2, 0, beside, 0),
        (3, 0, twin, 0),
        (3, 1, twin, 0),
    ):
        send(0, here, part, kind, to, at, local.at[part])
    size = qkv_ref.shape[2]
    load = pltpu.make_async_copy(qkv_ref.at[layer, 0], weight.at[pl.ds(0, size)], own_sem.at[1])
    load.start()
    weight[size:] = jnp.broadcast_to(rate_ref[layer], (weight.shape[0] - size, weight.shape[1]))
    arrive(0, across, 1)
    send(0, across, 1, 0, up, spot(-1))
    send(0, across, 1, 1, down, spot(1))
    send(0, across, 1, 3, twin)
    arrive(0, across, 0)
    send(0, across, 0, 3, twin)
    load.wait()
    own.wait()

    def project(places, offsets):
        for at in places:
            for x_ in (0, 1):
                arrive(at, 2 * x_ + 1 - core, 0)
                arrive(at, 2 * x_ + 1 - core, 1)
        count = len(places)
        block = full[places[0] : places[0] + count]
        rows = block.shape[1] * block.shape[2] * block.shape[3]
        out = dot(block.reshape(count * rows, block.shape[4]), weight[...], NT)
        out = out.reshape(count, 2, 2, *mixed.shape[1:])
        for i, off in enumerate(offsets):
            for x_ in (0, 1):
                mixed[pl.ds(name(x_, z + off, 0), 2)] = out[i, x_]

    def hand_over(k):
        for off in (k, -k) if k < last else (k,):
            arrive(spot(off), across, 0)
            send(spot(off), across, 0, 3, twin)

    def project_at(k):
        if k == 1:
            project((0,), (0,))
        if k < last:
            project((2 * k - 1, 2 * k), (k, -k))
        else:
            project((2 * k - 1,), (k,))

    turn = 1 - 2 * core
    for k in range(1, last + 1):
        ways = ((1, up, 0), (-1, down, 1)) if k < last else ((1, None, 0),)
        for which, part in ((here, 0), (here, 1), (across, 1)):
            for sign, to, kind in ways:
                at = spot(-sign * k)
                arrive(at, which, part)
                if k < last - 1:
                    send(at, which, part, kind, to, spot(-sign * (k + 1)))
                if part == 0:
                    send(at, which, 0, 2, beside)
                send(at, which, part, 3, twin)
        if k == last - 1:
            to = name(x, z + turn, core)
            at = spot(k) + 1 - core
            for which, part in ((here, 0), (here, 1), (across, 1)):
                send(at, which, part, 0, to, spot(last))
        if k > 1:
            hand_over(k - 1)
        if k > 2:
            project_at(k - 2)
    project_at(last - 1)
    hand_over(last)
    project_at(last)
    for copy in started:
        copy.wait_send()


class Exchange:
    def __init__(self, heads, shards, seqs, o, blocks, joined, sem_a, sem_b, sem_c, sem_d):
        self.heads, self.shards, self.seqs = heads, shards, seqs
        self.o, self.blocks, self.joined = o, blocks, joined
        self.sem_a, self.sem_b, self.sem_c, self.sem_d = sem_a, sem_b, sem_c, sem_d
        self.copies = shards // seqs
        self.index, self.head = lax.axis_index("seq"), lax.axis_index("head")
        self.slot = lax.div(self.head, self.copies)
        self.place = self.place_of(self.index)

    def place_of(self, index):
        return lax.rem(index, self.copies) * self.seqs + lax.div(index, self.copies)

    def first(self, t):
        there = lax.rem(self.head + t, self.heads)
        return remote(
            self.o.at[there],
            self.blocks.at[self.slot],
            self.sem_a.at[t],
            self.sem_b.at[self.slot],
            {"head": there},
        )

    def begin(self, outs, start):
        rows = self.o.shape[1] // outs.shape[2]
        self.o[...] = outs[:, start : start + rows].reshape(self.o.shape).astype(BF)
        pltpu.make_async_copy(
            self.o.at[self.head], self.blocks.at[self.slot], self.sem_b.at[self.slot]
        ).start()
        lax.fori_loop(1, self.heads, lambda t, c: (self.first(t).start(), c)[1], 0)

    def second(self, t):
        there = lax.rem(self.index + t, self.shards)
        spot = self.joined.at[self.place]
        return remote(spot, spot, self.sem_c.at[t], self.sem_d.at[self.place], {"seq": there})

    def go_on(self):
        count = self.blocks.shape[0]
        for i in range(count):
            pltpu.make_async_copy(self.o.at[0], self.blocks.at[i], self.sem_b.at[i]).wait()
        self.joined[self.place] = jnp.concatenate([self.blocks[i] for i in range(count)], 1)
        for t in range(1, self.shards):
            self.second(t).start()

    def finish(self):
        for t in range(1, self.shards):
            came = self.place_of(lax.rem(self.index + self.shards - t, self.shards))
            spot = self.joined.at[came]
            pltpu.make_async_copy(spot, spot, self.sem_d.at[came]).wait()

    def settle(self, active):
        for t in range(1, self.shards):
            self.second(t).wait_send()

        @pl.when(active)
        def _():
            lax.fori_loop(1, self.heads, lambda t, c: (self.first(t).wait_send(), c)[1], 0)


def out_phase(
    shards,
    seqs,
    portions,
    starts,
    outs,
    w_ref,
    local_ref,
    result,
    delta,
    parts,
    sem_e,
    sem_f,
):
    copies = shards // seqs
    index, head = lax.axis_index("seq"), lax.axis_index("head")
    active = lax.rem(index, copies) == lax.rem(head, copies)
    late = portions[1]

    @pl.when(active)
    def _():
        late.begin(outs, starts[1])

    def product(portion, start):
        portion.finish()
        joined = portion.joined
        rows, inner = joined.shape[1:]
        total = sum(
            jnp.dot(
                joined[pl.ds(i * seqs, seqs)].reshape(seqs * rows, inner),
                w_ref[i].reshape(inner, w_ref.shape[3]),
                preferred_element_type=F32,
            )
            for i in range(copies)
        )
        count = rows // delta.shape[2]
        delta[:, start : start + count] = total.reshape(seqs, count, *delta.shape[2:])

    product(portions[0], starts[0])
    late.go_on()
    product(late, starts[1])

    mine = pltpu.make_async_copy(delta.at[:, index], parts.at[index], sem_f.at[index])
    mine.start()
    sends = []
    for t in range(1, shards):
        there = lax.rem(index + t, shards)
        copy = remote(
            delta.at[:, there], parts.at[index], sem_e.at[t], sem_f.at[index], {"seq": there}
        )
        copy.start()
        sends.append(copy)
    for i in range(shards):
        pltpu.make_async_copy(delta.at[:, 0], parts.at[i], sem_f.at[i]).wait()
    cut = parts.shape[3]
    for i in range(shards):
        columns = slice(i * cut, (i + 1) * cut)
        summed = local_ref[:, :, columns].astype(F32) + parts[i].reshape(
            result.shape[0], result.shape[1], cut
        )
        result[:, :, columns] = summed.astype(BF)
    for copy in sends:
        copy.wait_send()
    for portion in portions:
        portion.settle(active)


def whole_kernel(heads, shards, seqs, counts, *refs):
    local, qkv_ref, rate_ref, weight_ref, *params = refs[:10]
    result = refs[10]
    rest = list(refs[11:])

    def take(count):
        taken = rest[:count]
        del rest[:count]
        return taken

    weight, outs, middle, load_sem = take(4)
    held = take(len(params))
    state = take(counts[0])
    loads = [
        pltpu.make_async_copy(src, dst, load_sem.at[i])
        for i, (src, dst) in enumerate(zip(params, held))
    ]
    for load in loads:
        load.start()
    greet(others("head", heads) + others("seq", shards))
    for layer in range(2):
        mixed, *gather = take(counts[1])
        sliced, *scan = take(counts[2])
        portions = [Exchange(heads, shards, seqs, *take(counts[3])) for _ in range(2)]
        out = take(counts[4])
        starts = (0, EARLY) if layer == 0 else (shards - EARLY, 0)
        source, target = (local, middle) if layer == 0 else (middle, result)
        full, *sems = gather
        gather_project(layer, source, qkv_ref, rate_ref, mixed, full, weight, *sems)
        chain, *scan_sems = scan
        if layer == 0:
            for load in loads:
                load.wait()
        scan_phase(
            layer == 0,
            layer,
            shards,
            heads,
            mixed,
            weight_ref,
            *held,
            portions[0],
            starts[0],
            EARLY * (heads * local.shape[0] * local.shape[1] // seqs // MINI) + 1,
            sliced,
            chain,
            outs,
            *scan_sems,
            *state,
        )
        out_phase(shards, seqs, portions, starts, outs, sliced, source, target, *out)


def body(tokens, qkv_weight, rate_weight, *rest):
    *params, out_weight = rest
    seqs, rows, width = tokens.shape
    heads, shards = lax.axis_size("head"), lax.axis_size("seq")
    hidden = params[0].shape[3]
    size = HEAD_SIZE
    lanes = 2 * MINI
    copies = shards // seqs
    minis = heads * rows // MINI
    cut = width // shards
    count = heads // copies
    dma = pltpu.SemaphoreType.DMA
    pair = lambda shape: [pltpu.VMEM(shape, BF)] * 2
    local = tokens.reshape(2, seqs * rows // 2, width)
    params[2] = params[2].transpose(0, 1, 3, 2)
    state = [
        pltpu.VMEM((hidden, lanes), F32),
        pltpu.VMEM((hidden, lanes), F32),
        pltpu.VMEM((size, hidden), F32),
        pltpu.VMEM((hidden, lanes), F32),
        pltpu.VMEM((size, lanes), F32),
        *pair((hidden, lanes)),
        *pair((size, lanes)),
        *pair((hidden, lanes)),
        *pair((size, lanes)),
    ]
    gather = [
        pltpu.VMEM((heads, seqs, rows, 4 * size), F32),
        pltpu.VMEM((heads // 4, 4, *local.shape), BF),
        dma((2,)),
        dma((4, heads // 4, 4, 2)),
        dma((heads // 4, 4, 2)),
    ]
    scan = [
        pltpu.VMEM((copies, count, size, cut), BF),
        pltpu.VMEM((shards * heads, rows, 4 * size), F32),
        dma((seqs, minis)),
        dma((shards * minis,)),
        dma((4, 2, count)),
        dma((2, count)),
    ]
    portion = lambda many: [
        pltpu.VMEM((heads, many * rows, size), BF),
        pltpu.VMEM((count, many * rows, size), BF),
        pltpu.VMEM((shards, many * rows, count * size), BF),
        dma((heads,)),
        dma((count,)),
        dma((shards,)),
        dma((shards,)),
    ]
    out = [
        pltpu.VMEM((seqs, shards, rows, cut), F32),
        pltpu.VMEM((shards, seqs, rows, cut), F32),
        dma((shards,)),
        dma((shards,)),
    ]
    layer = gather + scan + portion(EARLY) + portion(shards - EARLY) + out
    hbm = pl.BlockSpec(memory_space=pltpu.HBM)
    vmem = pl.BlockSpec(memory_space=pltpu.VMEM)
    counts = (len(state), len(gather), len(scan), len(portion(1)), len(out))
    result = pl.pallas_call(
        functools.partial(whole_kernel, heads, shards, seqs, counts),
        out_shape=jax.ShapeDtypeStruct(local.shape, BF),
        in_specs=[vmem, hbm, vmem, hbm] + [hbm] * 6,
        out_specs=vmem,
        scratch_shapes=[
            pltpu.VMEM((4 * size, width), BF),
            pltpu.VMEM((heads, shards, rows, size), F32),
            pltpu.VMEM(local.shape, BF),
            dma((len(params),)),
            *[pltpu.VMEM(param.shape, F32) for param in params],
            *state,
            *layer,
            *layer,
        ],
        compiler_params=pltpu.CompilerParams(
            vmem_limit_bytes=63 * 2**20, collective_id=0, has_side_effects=True
        ),
        name="two_layers",
    )(local, qkv_weight, rate_weight, out_weight, *params)
    return result.reshape(tokens.shape)


def solution(mesh):
    placed = (
        P(None, ("seq", "head"), None),
        P(None, "head", None, None),
        P(None, "head", None),
        P(None, "head", None, None),
        P(None, "head", None),
        P(None, "head", None, None),
        P(None, "head", None),
        P(None, "head", None),
        P(None, "head", None),
        P(None, "head", None),
    )
    return jax.shard_map(
        body, mesh=mesh, in_specs=placed, out_specs=P(None, ("seq", "head"), None), check_vma=False
    )
```
